32 devices in a mesh: row: 16 (over z, x, core), col: 2 (over y), chan: 1.
Axes of the slice: x: 2, y: 2, z: 4, core: 2. Of those that a mesh axis runs over, the one named last changes fastest.
Arguments:
- voltages: bfloat16 [128, 8, 137216], P('row', ('col', 'chan')), may hold values from -6 to 6
- lane_map: int32 [16, 2, 32], P('row', 'col'), may hold values from 0 to 31, each once within a row
- input_flags: int32 [128, 8], P('row', 'col'), may hold values 0 or 1
Outputs:
- visibility: bfloat16 [16, 2, 128, 8, 8, 128], P('chan', None, 'row', None, 'col')
The draws below stay inside these ranges and needn't reach their ends.
Inputs may be any that keep to these rules, and one draw needn't show every extreme that they name: For each block (row index, col index), lane_map lists every lane 0 to 31 once.
All inputs are finite; a program needn't handle non-finite values. No bound on the sum of `input_flags` on one device may be relied on, other than what follows from the above.
Results may differ from the reference program's by a relative error of at most 0.0069.
Values may be sent and summed in bfloat16 or wider, within the bound.
No kernel may reach another device: no remote copies, remote signals or barrier semaphores. Data moves between devices by JAX's collectives and lax.ppermute only.
A program may use at most 64 MiB of HBM per device.

```python
import jax
import jax.numpy as jnp
from jax import lax

NFFT = 2048
TAPS = 4
P_DEV = 8
Q_DEV = 4
SPECTRA = 64
NP = 128
NQ = 8
LANES = 32
CHANS = 16
FRAMES = 67
SAMPLES = 137216
N_ROW = 16
N_COL = 2


def place_ends(result, rng, low, largest):
    longest = result.shape.index(max(result.shape))
    spots = []
    for shift in (0, 1):
        where = [jax.random.randint(jax.random.fold_in(rng, axis), (), 0, length) for axis, length in enumerate(result.shape)]
        where[longest] = (where[longest] + shift) % result.shape[longest]
        spots.append(tuple(where))
    return result.at[spots[0]].set(low).at[spots[1]].set(largest)


def levels(own_key, extent, split, low, high):
    factor_of, own = 1.0, jax.random.fold_in(own_key, 6)
    for axis_at, parts in split:
        heights = jnp.exp(jax.random.uniform(jax.random.fold_in(own, axis_at), (parts,), jnp.float32, low / len(split), high / len(split)))
        factor_of = factor_of * jnp.repeat(heights, extent[axis_at] // parts).reshape([-1 if axis == axis_at else 1 for axis in range(len(extent))])
    return factor_of


def noise(key, dims, width, bound, shards=(), kind=jnp.bfloat16):
    factor_of = levels(key, dims, shards, -0.22, 0.18) if shards else 1.0
    result = jax.random.normal(key, dims, jnp.float32) * width * factor_of
    return jnp.minimum(jnp.maximum(result, -bound), bound).astype(kind)


def setup_inputs(seed: int = 0) -> dict:
    arg_keys = jax.random.split(jax.random.key(seed), 4)
    return {
        "voltages": noise(arg_keys[0], (NP, NQ, SAMPLES), 1.0, 6.0, ((0, 16), (1, 2))),
        "lane_map": jax.vmap(lambda own: jax.random.permutation(own, LANES))(jax.random.split(arg_keys[1], N_ROW * N_COL)).reshape((N_ROW, N_COL, LANES)).astype(jnp.int32),
        "input_flags": place_ends((jax.random.randint(arg_keys[2], (NP, NQ), 0, 8) < 7).astype(jnp.int32), jax.random.fold_in(arg_keys[2], 1), 0, 1),
    }


def kernel_table(nfft, taps, chans):
    length = taps * nfft
    position = jnp.arange(length, dtype=jnp.float32)
    centre = (position - length / 2 + 0.5) / nfft
    window = jnp.sinc(centre) * (0.5 - 0.5 * jnp.cos(2.0 * jnp.pi * (position + 0.5) / length))
    norm_scale = jnp.sqrt(2.0 / jnp.sum(window * window))
    window = (window * norm_scale).reshape(taps, nfft)
    sample = jnp.arange(nfft, dtype=jnp.int32)
    bin_index = nfft // 4 + jnp.arange(chans, dtype=jnp.int32)
    phase_index = bin_index[:, None] * sample[None, :] % nfft
    phases = phase_index.astype(jnp.float32) * (2.0 * jnp.pi / nfft)
    both_parts = jnp.stack([jnp.cos(phases).T, -jnp.sin(phases).T], -1)
    built = window.T[:, :, None, None] * both_parts[:, None, :, :]
    return built.reshape(nfft, taps * chans * 2).astype(jnp.bfloat16)

def one_channel(rows):
    real_part = rows[:, :SPECTRA]
    imag_part = rows[:, SPECTRA:]
    turned = jnp.concatenate([-imag_part, real_part], axis=-1)
    real_vis = jnp.dot(rows, rows.T, preferred_element_type=jnp.float32)
    imag_vis = jnp.dot(rows, turned.T, preferred_element_type=jnp.float32)
    stacked = (jnp.stack([real_vis, imag_vis]) * (1.0 / SPECTRA)).astype(jnp.bfloat16)
    return stacked.reshape(2, NP, NQ, NP, NQ).transpose(0, 1, 2, 4, 3)

def reference(voltages, lane_map, input_flags):
    table_rows = kernel_table(NFFT, TAPS, CHANS)
    frames = voltages.reshape(NP * NQ * FRAMES, NFFT)
    frame_sums = jnp.dot(frames, table_rows, preferred_element_type=jnp.float32)
    frame_sums = frame_sums.reshape(NP, NQ, FRAMES, TAPS, CHANS, 2)
    tap_sum = frame_sums[:, :, 0:SPECTRA, 0]
    for tap_idx in range(1, TAPS):
        tap_sum = tap_sum + frame_sums[:, :, tap_idx:tap_idx + SPECTRA, tap_idx]
    filtered = tap_sum.astype(jnp.bfloat16)
    blocks = filtered.reshape(N_ROW, P_DEV, N_COL, Q_DEV, SPECTRA, CHANS, 2)
    blocks = blocks.transpose(0, 2, 1, 3, 4, 5, 6).reshape(N_ROW, N_COL, LANES, SPECTRA, CHANS, 2)
    picked = jax.vmap(jax.vmap(lambda block_rows, lane_index: block_rows[lane_index]))(blocks, lane_map)
    picked = picked.reshape(N_ROW, N_COL, P_DEV, Q_DEV, SPECTRA, CHANS, 2)
    picked = picked.transpose(0, 2, 1, 3, 4, 5, 6).reshape(NP, NQ, SPECTRA, CHANS, 2)
    weights = input_flags.astype(jnp.float32)[:, :, None, None, None]
    channelised = (picked.astype(jnp.float32) * weights).astype(jnp.bfloat16)
    channel_major = channelised.transpose(3, 0, 1, 4, 2).reshape(CHANS, NP * NQ, 2 * SPECTRA)
    return lax.map(one_channel, channel_major)
```

```python
import jax
import jax.experimental.pallas as pl
import jax.experimental.pallas.tpu as pltpu
import jax.numpy as jnp
import ml_dtypes
import numpy as np
from jax import lax
from jax.sharding import PartitionSpec as P

NFFT = 2048
TAPS = 4
P_DEV = 8
Q_DEV = 4
CH_DEV = 16
SPECTRA = 64
LANES = 32
FRAMES = 67
CHUNK = 128
CHUNKS = NFFT // CHUNK
ROWS = 16


def kernel_table(nfft, taps, chans):
    length = taps * nfft
    position = jnp.arange(length, dtype=jnp.float32)
    centre = (position - length / 2 + 0.5) / nfft
    window = jnp.sinc(centre) * (0.5 - 0.5 * jnp.cos(2.0 * jnp.pi * (position + 0.5) / length))
    norm_scale = jnp.sqrt(2.0 / jnp.sum(window * window))
    window = (window * norm_scale).reshape(taps, nfft)
    sample = jnp.arange(nfft, dtype=jnp.int32)
    bin_index = nfft // 4 + jnp.arange(chans, dtype=jnp.int32)
    phase_index = bin_index[:, None] * sample[None, :] % nfft
    phases = phase_index.astype(jnp.float32) * (2.0 * jnp.pi / nfft)
    both_parts = jnp.stack([jnp.cos(phases).T, -jnp.sin(phases).T], -1)
    built = window.T[:, :, None, None] * both_parts[:, None, :, :]
    return built.reshape(nfft, taps * chans * 2).astype(jnp.bfloat16)


def per_device_general(voltages, lane_map, input_flags):
    all_chans = CH_DEV * lax.axis_size("chan")
    half_q = voltages.shape[1]
    table_rows = kernel_table(NFFT, TAPS, all_chans)
    frames = voltages.reshape(P_DEV, half_q, FRAMES, NFFT)
    frame_sums = jnp.einsum("pqfn,nk->pqfk", frames, table_rows, preferred_element_type=jnp.float32)
    frame_sums = frame_sums.reshape(P_DEV, half_q, FRAMES, TAPS, all_chans, 2)
    tap_sum = frame_sums[:, :, 0:SPECTRA, 0]
    for tap_idx in range(1, TAPS):
        tap_sum = tap_sum + frame_sums[:, :, tap_idx : tap_idx + SPECTRA, tap_idx]
    filtered = tap_sum.astype(jnp.bfloat16)
    filtered = filtered.transpose(3, 0, 1, 4, 2).reshape(all_chans, P_DEV, half_q, 2 * SPECTRA)
    turned_over = lax.all_to_all(filtered, "chan", split_axis=0, concat_axis=2, tiled=True)
    lane_rows = turned_over.reshape(CH_DEV, LANES, 2 * SPECTRA)
    lane_index = lane_map.reshape(LANES)
    selector = (lane_index[:, None] == jnp.arange(LANES, dtype=jnp.int32)[None, :]).astype(
        jnp.bfloat16
    )
    reordered = jnp.einsum("kl,clz->ckz", selector, lane_rows, preferred_element_type=jnp.float32)
    weights = input_flags.reshape(LANES).astype(jnp.float32)[None, :, None]
    channelised = (
        (reordered * weights).astype(jnp.bfloat16).reshape(CH_DEV, P_DEV, Q_DEV, 2 * SPECTRA)
    )
    row_group = lax.all_gather(channelised, "col", axis=2, tiled=True)
    grid_cols = row_group.shape[2]
    row_block = row_group.reshape(CH_DEV, P_DEV * grid_cols, 2 * SPECTRA)
    col_set = lax.all_gather(channelised, "row", axis=1, tiled=True)
    real_part = col_set[..., :SPECTRA]
    imag_part = col_set[..., SPECTRA:]
    turned = jnp.concatenate([-imag_part, real_part], axis=-1)
    col_block = jnp.stack([col_set, turned], axis=1)
    products = jnp.einsum(
        "cik,crpqk->criqp", row_block, col_block, preferred_element_type=jnp.float32
    )
    products = (products * (1.0 / SPECTRA)).astype(jnp.bfloat16)
    return products.reshape(CH_DEV, 2, P_DEV, grid_cols, Q_DEV, col_set.shape[1])


def filter_table(chans):
    f32 = np.float32
    length = TAPS * NFFT
    position = np.arange(length, dtype=f32)
    centre = (position - f32(length / 2) + f32(0.5)) / f32(NFFT)
    window = np.sinc(centre.astype(np.float64)).astype(f32)
    window = window * (f32(0.5) - f32(0.5) * np.cos(f32(2.0 * np.pi) * (position + f32(0.5)) / f32(length)))
    window = (window * np.sqrt(f32(2.0) / np.sum(window * window))).reshape(TAPS, NFFT)
    bins = NFFT // 4 + np.arange(chans)
    phase_index = np.arange(NFFT)[:, None] * bins[None, :] % NFFT
    phases = phase_index.astype(f32) * f32(2.0 * np.pi / NFFT)
    parts = np.stack([np.cos(phases), -np.sin(phases)], 1)
    table = window.T[:, :, None, None] * parts[:, None]
    table = table.reshape(CHUNKS // 2, 2, CHUNK, TAPS * 2 * chans)
    return table.transpose(0, 2, 1, 3).reshape(NFFT // 2, -1).astype(ml_dtypes.bfloat16)


def lane_order():
    order = np.zeros((8 * SPECTRA, 8 * SPECTRA), np.float32)
    part, s, half, q = np.meshgrid(range(2), range(SPECTRA // 2), range(2), range(Q_DEV), indexing="ij")
    source = ((part * (SPECTRA // 2) + s) * 2 + half) * Q_DEV + q
    target = ((q * 2 + part) * 2 + half) * (SPECTRA // 2) + s
    order[source.ravel(), target.ravel()] = 1
    return order.astype(ml_dtypes.bfloat16)


def filter_kernel(
    volts, table, order, lane_map, flags, out, held, table_v, order_v, sums, lanes, rows, in_sem, const_sem
):
    ahead = 3
    arrivals = [
        [
            pltpu.make_async_copy(volts.at[p, :, j], held.at[p, j, pl.ds(0, FRAMES)], in_sem.at[p])
            for j in range(CHUNKS // 2)
        ]
        for p in range(P_DEV)
    ]
    get_table = pltpu.make_async_copy(table, table_v, const_sem.at[0])
    get_order = pltpu.make_async_copy(order, order_v, const_sem.at[1])

    def begin(p):
        for copy in arrivals[p]:
            copy.start()
        if p == 0:
            get_table.start()
        if p == 2:
            get_order.start()

    first_half = lax.broadcasted_iota(jnp.int32, (35, 8, CHUNK), 1) < Q_DEV
    tap_of_lane = lax.broadcasted_iota(jnp.int32, (32, 8, CHUNK), 2) // 32

    def frames_of(p):
        block = jnp.concatenate(
            [held.at[p, j].reshape(68 * 8, CHUNK)[...] for j in range(CHUNKS // 2)], axis=1
        )
        both = jnp.dot(block, table_v[...], preferred_element_type=jnp.float32).reshape(68, 8, 2 * CHUNK)
        even, odd = both[:, :, :CHUNK], both[:, :, CHUNK:]
        straight = jnp.where(first_half, even[0:35], odd[32:67])
        crossed = jnp.where(first_half, even[32:67], odd[0:35])
        sums[p % 4] = straight + pltpu.roll(crossed, 4, 1)

    def finish(first):
        total = None
        for turn in range(4):
            term = sums[turn, 0:32]
            for tap in range(1, TAPS):
                term = jnp.where(tap_of_lane == tap, sums[(tap + turn) % 4, tap : tap + 32], term)
            if turn:
                term = pltpu.roll(term, 32 * turn, 2)
            total = term if total is None else total + term
        filtered = total.reshape(4 * SPECTRA, CHUNK).T.astype(jnp.bfloat16)
        filtered = filtered.reshape(4, 2, CH_DEV, 4 * SPECTRA)
        filtered = jnp.concatenate(
            [jnp.concatenate([filtered[i, 0], filtered[i, 1]], axis=1) for i in range(4)], axis=0
        )
        ordered = jnp.dot(filtered, order_v[...], preferred_element_type=jnp.float32)
        for i in range(4):
            for q in range(Q_DEV):
                lanes[(first + i) * Q_DEV + q] = ordered[i * 16 : i * 16 + 16, q * 128 : q * 128 + 128]

    for p in range(ahead):
        begin(p)
    for p in range(P_DEV):
        for copy in arrivals[p]:
            copy.wait()
        if p + ahead < P_DEV:
            begin(p + ahead)
        if p == 0:
            get_table.wait()
        frames_of(p)
        if p % 4 == 3:
            if p == 3:
                get_order.wait()
            finish(p - 3)
    for p in range(P_DEV):
        for q in range(Q_DEV):
            weight = flags[q, p].astype(jnp.float32)
            rows[pl.ds(q * P_DEV + p, CH_DEV, stride=LANES), :] = lanes[lane_map[0, p * Q_DEV + q]] * weight
    out[...] = rows[...].astype(jnp.bfloat16).reshape(CH_DEV, LANES, 2 * SPECTRA)


def channelise(voltages, lane_map, input_flags):
    volts = voltages.reshape(P_DEV, Q_DEV, FRAMES, CHUNKS // 2, 2, CHUNK).transpose(0, 2, 3, 4, 1, 5)
    volts = volts.reshape(P_DEV, FRAMES, CHUNKS // 2, 2 * Q_DEV, CHUNK)
    vmem = pl.BlockSpec(memory_space=pltpu.VMEM)
    smem = pl.BlockSpec(memory_space=pltpu.SMEM)
    hbm = pl.BlockSpec(memory_space=pltpu.HBM)
    return pl.pallas_call(
        filter_kernel,
        out_shape=jax.ShapeDtypeStruct((CH_DEV, LANES, 2 * SPECTRA), jnp.bfloat16),
        in_specs=[hbm, hbm, hbm, smem, smem],
        out_specs=vmem,
        scratch_shapes=[
            pltpu.VMEM((P_DEV, CHUNKS // 2, 68, 2 * Q_DEV, CHUNK), jnp.bfloat16),
            pltpu.VMEM((NFFT // 2, 2 * CHUNK), jnp.bfloat16),
            pltpu.VMEM((8 * SPECTRA, 8 * SPECTRA), jnp.bfloat16),
            pltpu.VMEM((4, 35, 8, CHUNK), jnp.float32),
            pltpu.VMEM((LANES, CH_DEV, 2 * SPECTRA), jnp.float32),
            pltpu.VMEM((CH_DEV * LANES, 2 * SPECTRA), jnp.float32),
            pltpu.SemaphoreType.DMA((P_DEV,)),
            pltpu.SemaphoreType.DMA((2,)),
        ],
        compiler_params=pltpu.CompilerParams(vmem_limit_bytes=56 << 20),
        name="channelise",
    )(
        volts,
        jnp.asarray(filter_table(CH_DEV)),
        jnp.asarray(lane_order()),
        lane_map.reshape(1, LANES),
        input_flags.T,
    )


def gather_rows(own):
    def swap(block, d):
        return lax.ppermute(block, "row", [(i, i ^ d) for i in range(ROWS)])

    blocks = {0: own}
    blocks[8] = swap(own, 8)
    blocks[4] = swap(own, 4)
    blocks[2] = swap(own, 2)
    blocks[12] = swap(blocks[8], 4)
    for d in (4, 8, 12):
        blocks[d + 2] = swap(blocks[d], 2)
    for d in range(0, ROWS, 2):
        blocks[d + 1] = swap(blocks[d], 1)
    return [blocks[d] for d in range(ROWS)]


def correlate_kernel(*refs):
    blocks, other = refs[:ROWS], refs[ROWS]
    out, columns, spread, packed, sem = refs[ROWS + 1 :]
    row = lax.axis_index("row")
    first_col = lax.axis_index("col") == 0
    odd = lax.rem(row, 2) == 1
    pair = lax.div(row, 2)
    sign = jnp.where(lax.broadcasted_iota(jnp.int32, (64, 128), 1) < SPECTRA, 1.0, -1.0)
    sign = sign.astype(jnp.bfloat16)
    copies = []
    for c in range(CH_DEV):
        slot = c % 2
        for e in range(ROWS // 2):
            near, far = blocks[2 * e][c], blocks[2 * e + 1][c]
            low, high = jnp.where(odd, far, near), jnp.where(odd, near, far)
            at = pl.multiple_of(lax.bitwise_xor(pair, e) * 16, 16)
            for q in range(Q_DEV):
                both = jnp.concatenate([low[q * 8 : q * 8 + 8], high[q * 8 : q * 8 + 8]], axis=0)
                columns[slot, q, pl.ds(at, 16), :] = both
        mine, theirs = blocks[0][c], other[c]
        left = jnp.concatenate(
            [jnp.where(first_col, mine, theirs), jnp.where(first_col, theirs, mine)], axis=0
        )
        left = jnp.concatenate([left, pltpu.roll(left, SPECTRA, 1) * sign], axis=0)
        for h in range(2):
            right = columns[slot, 2 * h : 2 * h + 2].reshape(256, 2 * SPECTRA)
            products = lax.dot_general(
                left, right, (((1,), (1,)), ((), ())), preferred_element_type=jnp.float32
            ) * (1.0 / SPECTRA)
            for k in range(2):
                for part in range(2):
                    for q in range(2 * Q_DEV):
                        start = (part * 8 + q) * 8
                        spread[slot, part, pl.ds(q * Q_DEV + 2 * h + k, 8, stride=32), :] = products[
                            start : start + 8, k * 128 : k * 128 + 128
                        ]
        packed[c] = spread[slot].astype(jnp.bfloat16)
        copy = pltpu.make_async_copy(packed.at[c], out.at[c], sem.at[c])
        copy.start()
        copies.append(copy)
    for copy in copies:
        copy.wait()


def correlate(blocks, other):
    vmem = pl.BlockSpec(memory_space=pltpu.VMEM)
    return pl.pallas_call(
        correlate_kernel,
        out_shape=jax.ShapeDtypeStruct((CH_DEV, 2, 2 * LANES * Q_DEV, 8 * ROWS), jnp.bfloat16),
        in_specs=[vmem] * (ROWS + 1),
        out_specs=pl.BlockSpec(memory_space=pltpu.HBM),
        scratch_shapes=[
            pltpu.VMEM((2, Q_DEV, 8 * ROWS, 2 * SPECTRA), jnp.bfloat16),
            pltpu.VMEM((2, 2, 2 * LANES * Q_DEV, 8 * ROWS), jnp.float32),
            pltpu.VMEM((CH_DEV, 2, 2 * LANES * Q_DEV, 8 * ROWS), jnp.bfloat16),
            pltpu.SemaphoreType.DMA((CH_DEV,)),
        ],
        compiler_params=pltpu.CompilerParams(vmem_limit_bytes=32 << 20),
        name="correlate",
    )(*blocks, other)


def per_device(voltages, lane_map, input_flags):
    own = channelise(voltages, lane_map, input_flags)
    other = lax.ppermute(own, "col", [(0, 1), (1, 0)])
    products = correlate(gather_rows(own), other)
    return products.reshape(CH_DEV, 2, P_DEV, 2 * Q_DEV, Q_DEV, P_DEV * ROWS)


def solution(mesh):
    fast = mesh.shape["row"] == ROWS and mesh.shape["col"] == 2 and mesh.shape["chan"] == 1
    return jax.shard_map(
        per_device if fast else per_device_general,
        mesh=mesh,
        in_specs=(P("row", ("col", "chan"), None), P("row", "col", None), P("row", "col")),
        out_specs=P("chan", None, "row", None, "col", None),
        check_vma=False,
    )
```

```python
import jax
import jax.experimental.pallas as pl
import jax.experimental.pallas.tpu as pltpu
import jax.numpy as jnp
import ml_dtypes
import numpy as np
from jax import lax
from jax.sharding import PartitionSpec as P

NFFT = 2048
TAPS = 4
P_DEV = 8
Q_DEV = 4
CH_DEV = 16
SPECTRA = 64
LANES = 32
FRAMES = 67
CHUNK = 128
CHUNKS = NFFT // CHUNK
ROWS = 16


def kernel_table(nfft, taps, chans):
    length = taps * nfft
    position = jnp.arange(length, dtype=jnp.float32)
    centre = (position - length / 2 + 0.5) / nfft
    window = jnp.sinc(centre) * (0.5 - 0.5 * jnp.cos(2.0 * jnp.pi * (position + 0.5) / length))
    norm_scale = jnp.sqrt(2.0 / jnp.sum(window * window))
    window = (window * norm_scale).reshape(taps, nfft)
    sample = jnp.arange(nfft, dtype=jnp.int32)
    bin_index = nfft // 4 + jnp.arange(chans, dtype=jnp.int32)
    phase_index = bin_index[:, None] * sample[None, :] % nfft
    phases = phase_index.astype(jnp.float32) * (2.0 * jnp.pi / nfft)
    both_parts = jnp.stack([jnp.cos(phases).T, -jnp.sin(phases).T], -1)
    built = window.T[:, :, None, None] * both_parts[:, None, :, :]
    return built.reshape(nfft, taps * chans * 2).astype(jnp.bfloat16)


def per_device_general(voltages, lane_map, input_flags):
    all_chans = CH_DEV * lax.axis_size("chan")
    half_q = voltages.shape[1]
    table_rows = kernel_table(NFFT, TAPS, all_chans)
    frames = voltages.reshape(P_DEV, half_q, FRAMES, NFFT)
    frame_sums = jnp.einsum("pqfn,nk->pqfk", frames, table_rows, preferred_element_type=jnp.float32)
    frame_sums = frame_sums.reshape(P_DEV, half_q, FRAMES, TAPS, all_chans, 2)
    tap_sum = frame_sums[:, :, 0:SPECTRA, 0]
    for tap_idx in range(1, TAPS):
        tap_sum = tap_sum + frame_sums[:, :, tap_idx : tap_idx + SPECTRA, tap_idx]
    filtered = tap_sum.astype(jnp.bfloat16)
    filtered = filtered.transpose(3, 0, 1, 4, 2).reshape(all_chans, P_DEV, half_q, 2 * SPECTRA)
    turned_over = lax.all_to_all(filtered, "chan", split_axis=0, concat_axis=2, tiled=True)
    lane_rows = turned_over.reshape(CH_DEV, LANES, 2 * SPECTRA)
    lane_index = lane_map.reshape(LANES)
    selector = (lane_index[:, None] == jnp.arange(LANES, dtype=jnp.int32)[None, :]).astype(
        jnp.bfloat16
    )
    reordered = jnp.einsum("kl,clz->ckz", selector, lane_rows, preferred_element_type=jnp.float32)
    weights = input_flags.reshape(LANES).astype(jnp.float32)[None, :, None]
    channelised = (
        (reordered * weights).astype(jnp.bfloat16).reshape(CH_DEV, P_DEV, Q_DEV, 2 * SPECTRA)
    )
    row_group = lax.all_gather(channelised, "col", axis=2, tiled=True)
    grid_cols = row_group.shape[2]
    row_block = row_group.reshape(CH_DEV, P_DEV * grid_cols, 2 * SPECTRA)
    col_set = lax.all_gather(channelised, "row", axis=1, tiled=True)
    real_part = col_set[..., :SPECTRA]
    imag_part = col_set[..., SPECTRA:]
    turned = jnp.concatenate([-imag_part, real_part], axis=-1)
    col_block = jnp.stack([col_set, turned], axis=1)
    products = jnp.einsum(
        "cik,crpqk->criqp", row_block, col_block, preferred_element_type=jnp.float32
    )
    products = (products * (1.0 / SPECTRA)).astype(jnp.bfloat16)
    return products.reshape(CH_DEV, 2, P_DEV, grid_cols, Q_DEV, col_set.shape[1])


def filter_table(chans):
    f32 = np.float32
    length = TAPS * NFFT
    position = np.arange(length, dtype=f32)
    centre = (position - f32(length / 2) + f32(0.5)) / f32(NFFT)
    window = np.sinc(centre.astype(np.float64)).astype(f32)
    window = window * (f32(0.5) - f32(0.5) * np.cos(f32(2.0 * np.pi) * (position + f32(0.5)) / f32(length)))
    window = (window * np.sqrt(f32(2.0) / np.sum(window * window))).reshape(TAPS, NFFT)
    bins = NFFT // 4 + np.arange(chans)
    phase_index = np.arange(NFFT)[:, None] * bins[None, :] % NFFT
    phases = phase_index.astype(f32) * f32(2.0 * np.pi / NFFT)
    parts = np.stack([np.cos(phases), -np.sin(phases)], 1)
    table = window.T[:, :, None, None] * parts[:, None]
    table = table.reshape(CHUNKS // 2, 2, CHUNK, TAPS * 2 * chans)
    return table.transpose(0, 2, 1, 3).reshape(NFFT // 2, -1).astype(ml_dtypes.bfloat16)


def filter_kernel(
    volts, table, lane_map, flags, out, held, table_v, map_s, flags_s, frames, sums, lanes, rows, in_sem, const_sem
):
    ahead = 3
    arrivals = [
        [
            pltpu.make_async_copy(volts.at[p, :, j], held.at[p, j, pl.ds(0, FRAMES)], in_sem.at[p])
            for j in range(CHUNKS // 2)
        ]
        for p in range(P_DEV)
    ]
    get_table = pltpu.make_async_copy(table, table_v, const_sem.at[0])
    get_map = pltpu.make_async_copy(lane_map, map_s, const_sem.at[1])
    get_flags = pltpu.make_async_copy(flags, flags_s, const_sem.at[2])

    def begin(p):
        for copy in arrivals[p]:
            copy.start()
        if p == 0:
            get_table.start()
        if p == 2:
            get_map.start()
            get_flags.start()

    first_half = lax.broadcasted_iota(jnp.int32, (8, 8, CHUNK), 1) < Q_DEV
    real_lanes = lax.broadcasted_iota(jnp.int32, (CH_DEV, 2 * SPECTRA), 1) < SPECTRA
    lane_group = lax.broadcasted_iota(jnp.int32, (64, CHUNK), 1) // 32

    def pair(low, high):
        upper = first_half[: low.shape[0]]
        straight = jnp.where(upper, low[:, :, :CHUNK], high[:, :, CHUNK:])
        crossed = jnp.where(upper, high[:, :, :CHUNK], low[:, :, CHUNK:])
        return straight + pltpu.roll(crossed, 4, 1)

    def frames_of(p, i, kept):
        spans = [(64 * i, 64), (256 + 64 * i, 64 if i < 3 else 96)]
        block = jnp.concatenate(
            [
                jnp.concatenate([held.at[p, j].reshape(68 * 8, CHUNK)[at : at + size] for at, size in spans], axis=0)
                for j in range(CHUNKS // 2)
            ],
            axis=1,
        )
        both = jnp.dot(block, table_v[...], preferred_element_type=jnp.float32)
        both = both.reshape(-1, 8, 2 * CHUNK)
        frames[p % 2, 8 * i : 8 * i + 8] = pair(both[:8], both[8:16])
        if i == 0:
            return both[8:11]
        if i == 3:
            frames[p % 2, 32:35] = pair(kept, both[16:19])
        return kept

    def taps_of(p, i):
        total = None
        for tap in range(TAPS):
            term = frames[p % 2, 8 * i + tap : 8 * i + tap + 8]
            turn = 32 * (p % 4 - tap) % CHUNK
            if turn:
                term = pltpu.roll(term, turn, 2)
            total = term if total is None else total + term
        total = total.reshape(64, CHUNK)
        at = slice(64 * i, 64 * i + 64)
        sums[p // 4, at] = total if p % 4 == 0 else jnp.where(lane_group == p % 4, total, sums[p // 4, at])

    def finish(first):
        by_q = [
            sums[first // 4, pl.ds(half * Q_DEV + q, SPECTRA // 2, stride=8), :]
            for q in range(Q_DEV)
            for half in range(2)
        ]
        turned = jnp.concatenate(by_q, axis=0).T.reshape(4, 2, CH_DEV, Q_DEV * SPECTRA)
        for i in range(4):
            for q in range(Q_DEV):
                real, imag = (turned[i, part, :, q // 2 * CHUNK : q // 2 * CHUNK + CHUNK] for part in range(2))
                if q % 2:
                    real = pltpu.roll(real, SPECTRA, 1)
                else:
                    imag = pltpu.roll(imag, SPECTRA, 1)
                lanes[(first + i) * Q_DEV + q] = jnp.where(real_lanes, real, imag)

    for p in range(ahead):
        begin(p)
    for p in range(P_DEV):
        for copy in arrivals[p]:
            copy.wait()
        if p + ahead < P_DEV:
            begin(p + ahead)
        if p == 0:
            get_table.wait()
        if p == 5:
            get_map.wait()
            get_flags.wait()
        kept = None
        for i in range(4):
            kept = frames_of(p, i, kept)
            if p > 0:
                taps_of(p - 1, i)
        if p == 5:
            finish(0)
    for i in range(4):
        taps_of(P_DEV - 1, i)
    finish(4)
    for p in range(P_DEV):
        for q in range(Q_DEV):
            weight = flags_s[q, p].astype(jnp.float32)
            rows[pl.ds(q * P_DEV + p, CH_DEV, stride=LANES), :] = lanes[map_s[0, p * Q_DEV + q]] * weight
    out[...] = rows[...].astype(jnp.bfloat16).reshape(CH_DEV, LANES, 2 * SPECTRA)


def channelise(voltages, lane_map, input_flags):
    volts = voltages.reshape(P_DEV, Q_DEV, FRAMES, CHUNKS // 2, 2, CHUNK).transpose(0, 2, 3, 4, 1, 5)
    volts = volts.reshape(P_DEV, FRAMES, CHUNKS // 2, 2 * Q_DEV, CHUNK)
    vmem = pl.BlockSpec(memory_space=pltpu.VMEM)
    hbm = pl.BlockSpec(memory_space=pltpu.HBM)
    return pl.pallas_call(
        filter_kernel,
        out_shape=jax.ShapeDtypeStruct((CH_DEV, LANES, 2 * SPECTRA), jnp.bfloat16),
        in_specs=[hbm] * 4,
        out_specs=vmem,
        scratch_shapes=[
            pltpu.VMEM((P_DEV, CHUNKS // 2, 68, 2 * Q_DEV, CHUNK), jnp.bfloat16),
            pltpu.VMEM((NFFT // 2, 2 * CHUNK), jnp.bfloat16),
            pltpu.SMEM((1, LANES), jnp.int32),
            pltpu.SMEM((Q_DEV, P_DEV), jnp.int32),
            pltpu.VMEM((2, 35, 8, CHUNK), jnp.float32),
            pltpu.VMEM((2, 4 * SPECTRA, CHUNK), jnp.float32),
            pltpu.VMEM((LANES, CH_DEV, 2 * SPECTRA), jnp.float32),
            pltpu.VMEM((CH_DEV * LANES, 2 * SPECTRA), jnp.float32),
            pltpu.SemaphoreType.DMA((P_DEV,)),
            pltpu.SemaphoreType.DMA((3,)),
        ],
        compiler_params=pltpu.CompilerParams(vmem_limit_bytes=56 << 20),
        name="channelise",
    )(
        volts,
        jnp.asarray(filter_table(CH_DEV)),
        lane_map.reshape(1, LANES),
        input_flags.T,
    )


def gather_rows(own):
    def swap(block, d):
        return lax.ppermute(block, "row", [(i, i ^ d) for i in range(ROWS)])

    blocks = {0: own}
    blocks[8] = swap(own, 8)
    blocks[4] = swap(own, 4)
    blocks[2] = swap(own, 2)
    blocks[12] = swap(blocks[8], 4)
    for d in (4, 8, 12):
        blocks[d + 2] = swap(blocks[d], 2)
    for d in range(0, ROWS, 2):
        blocks[d + 1] = swap(blocks[d], 1)
    return [blocks[d] for d in range(ROWS)]


def correlate_kernel(*refs):
    blocks, other = refs[:ROWS], refs[ROWS]
    out, columns, spread, packed, sem = refs[ROWS + 1 :]
    row = lax.axis_index("row")
    first_col = lax.axis_index("col") == 0
    odd = lax.rem(row, 2) == 1
    pair = lax.div(row, 2)
    sign = jnp.where(lax.broadcasted_iota(jnp.int32, (64, 128), 1) < SPECTRA, 1.0, -1.0)
    sign = sign.astype(jnp.bfloat16)
    copies = []
    for c in range(CH_DEV):
        slot = c % 2
        for e in range(ROWS // 2):
            near, far = blocks[2 * e][c], blocks[2 * e + 1][c]
            low, high = jnp.where(odd, far, near), jnp.where(odd, near, far)
            at = pl.multiple_of(lax.bitwise_xor(pair, e) * 16, 16)
            for q in range(Q_DEV):
                both = jnp.concatenate([low[q * 8 : q * 8 + 8], high[q * 8 : q * 8 + 8]], axis=0)
                columns[slot, q, pl.ds(at, 16), :] = both
        mine, theirs = blocks[0][c], other[c]
        left = jnp.concatenate(
            [jnp.where(first_col, mine, theirs), jnp.where(first_col, theirs, mine)], axis=0
        )
        left = jnp.concatenate([left, pltpu.roll(left, SPECTRA, 1) * sign], axis=0)
        for h in range(2):
            right = columns[slot, 2 * h : 2 * h + 2].reshape(256, 2 * SPECTRA)
            products = lax.dot_general(
                left, right, (((1,), (1,)), ((), ())), preferred_element_type=jnp.float32
            ) * (1.0 / SPECTRA)
            for k in range(2):
                for part in range(2):
                    for q in range(2 * Q_DEV):
                        start = (part * 8 + q) * 8
                        spread[slot, part, pl.ds(q * Q_DEV + 2 * h + k, 8, stride=32), :] = products[
                            start : start + 8, k * 128 : k * 128 + 128
                        ]
        packed[c] = spread[slot].astype(jnp.bfloat16)
        copy = pltpu.make_async_copy(packed.at[c], out.at[c], sem.at[c])
        copy.start()
        copies.append(copy)
    for copy in copies:
        copy.wait()


def correlate(blocks, other):
    vmem = pl.BlockSpec(memory_space=pltpu.VMEM)
    return pl.pallas_call(
        correlate_kernel,
        out_shape=jax.ShapeDtypeStruct((CH_DEV, 2, 2 * LANES * Q_DEV, 8 * ROWS), jnp.bfloat16),
        in_specs=[vmem] * (ROWS + 1),
        out_specs=pl.BlockSpec(memory_space=pltpu.HBM),
        scratch_shapes=[
            pltpu.VMEM((2, Q_DEV, 8 * ROWS, 2 * SPECTRA), jnp.bfloat16),
            pltpu.VMEM((2, 2, 2 * LANES * Q_DEV, 8 * ROWS), jnp.float32),
            pltpu.VMEM((CH_DEV, 2, 2 * LANES * Q_DEV, 8 * ROWS), jnp.bfloat16),
            pltpu.SemaphoreType.DMA((CH_DEV,)),
        ],
        compiler_params=pltpu.CompilerParams(vmem_limit_bytes=32 << 20),
        name="correlate",
    )(*blocks, other)


def per_device(voltages, lane_map, input_flags):
    own = channelise(voltages, lane_map, input_flags)
    other = lax.ppermute(own, "col", [(0, 1), (1, 0)])
    products = correlate(gather_rows(own), other)
    return products.reshape(CH_DEV, 2, P_DEV, 2 * Q_DEV, Q_DEV, P_DEV * ROWS)


def solution(mesh):
    fast = mesh.shape["row"] == ROWS and mesh.shape["col"] == 2 and mesh.shape["chan"] == 1
    return jax.shard_map(
        per_device if fast else per_device_general,
        mesh=mesh,
        in_specs=(P("row", ("col", "chan"), None), P("row", "col", None), P("row", "col")),
        out_specs=P("chan", None, "row", None, "col", None),
        check_vma=False,
    )
```

```python
import jax
import jax.experimental.pallas as pl
import jax.experimental.pallas.tpu as pltpu
import jax.numpy as jnp
import ml_dtypes
import numpy as np
from jax import lax
from jax.sharding import PartitionSpec as P

NFFT = 2048
TAPS = 4
P_DEV = 8
Q_DEV = 4
CH_DEV = 16
SPECTRA = 64
LANES = 32
FRAMES = 67
CHUNK = 128
CHUNKS = NFFT // CHUNK
ROWS = 16


def kernel_table(nfft, taps, chans):
    length = taps * nfft
    position = jnp.arange(length, dtype=jnp.float32)
    centre = (position - length / 2 + 0.5) / nfft
    window = jnp.sinc(centre) * (0.5 - 0.5 * jnp.cos(2.0 * jnp.pi * (position + 0.5) / length))
    norm_scale = jnp.sqrt(2.0 / jnp.sum(window * window))
    window = (window * norm_scale).reshape(taps, nfft)
    sample = jnp.arange(nfft, dtype=jnp.int32)
    bin_index = nfft // 4 + jnp.arange(chans, dtype=jnp.int32)
    phase_index = bin_index[:, None] * sample[None, :] % nfft
    phases = phase_index.astype(jnp.float32) * (2.0 * jnp.pi / nfft)
    both_parts = jnp.stack([jnp.cos(phases).T, -jnp.sin(phases).T], -1)
    built = window.T[:, :, None, None] * both_parts[:, None, :, :]
    return built.reshape(nfft, taps * chans * 2).astype(jnp.bfloat16)


def per_device_general(voltages, lane_map, input_flags):
    all_chans = CH_DEV * lax.axis_size("chan")
    half_q = voltages.shape[1]
    table_rows = kernel_table(NFFT, TAPS, all_chans)
    frames = voltages.reshape(P_DEV, half_q, FRAMES, NFFT)
    frame_sums = jnp.einsum("pqfn,nk->pqfk", frames, table_rows, preferred_element_type=jnp.float32)
    frame_sums = frame_sums.reshape(P_DEV, half_q, FRAMES, TAPS, all_chans, 2)
    tap_sum = frame_sums[:, :, 0:SPECTRA, 0]
    for tap_idx in range(1, TAPS):
        tap_sum = tap_sum + frame_sums[:, :, tap_idx : tap_idx + SPECTRA, tap_idx]
    filtered = tap_sum.astype(jnp.bfloat16)
    filtered = filtered.transpose(3, 0, 1, 4, 2).reshape(all_chans, P_DEV, half_q, 2 * SPECTRA)
    turned_over = lax.all_to_all(filtered, "chan", split_axis=0, concat_axis=2, tiled=True)
    lane_rows = turned_over.reshape(CH_DEV, LANES, 2 * SPECTRA)
    lane_index = lane_map.reshape(LANES)
    selector = (lane_index[:, None] == jnp.arange(LANES, dtype=jnp.int32)[None, :]).astype(
        jnp.bfloat16
    )
    reordered = jnp.einsum("kl,clz->ckz", selector, lane_rows, preferred_element_type=jnp.float32)
    weights = input_flags.reshape(LANES).astype(jnp.float32)[None, :, None]
    channelised = (
        (reordered * weights).astype(jnp.bfloat16).reshape(CH_DEV, P_DEV, Q_DEV, 2 * SPECTRA)
    )
    row_group = lax.all_gather(channelised, "col", axis=2, tiled=True)
    grid_cols = row_group.shape[2]
    row_block = row_group.reshape(CH_DEV, P_DEV * grid_cols, 2 * SPECTRA)
    col_set = lax.all_gather(channelised, "row", axis=1, tiled=True)
    real_part = col_set[..., :SPECTRA]
    imag_part = col_set[..., SPECTRA:]
    turned = jnp.concatenate([-imag_part, real_part], axis=-1)
    col_block = jnp.stack([col_set, turned], axis=1)
    products = jnp.einsum(
        "cik,crpqk->criqp", row_block, col_block, preferred_element_type=jnp.float32
    )
    products = (products * (1.0 / SPECTRA)).astype(jnp.bfloat16)
    return products.reshape(CH_DEV, 2, P_DEV, grid_cols, Q_DEV, col_set.shape[1])


PITCH = 36


def filter_table(chans):
    f32 = np.float32
    length = TAPS * NFFT
    position = np.arange(length, dtype=f32)
    centre = (position - f32(length / 2) + f32(0.5)) / f32(NFFT)
    window = np.sinc(centre.astype(np.float64)).astype(f32)
    window = window * (f32(0.5) - f32(0.5) * np.cos(f32(2.0 * np.pi) * (position + f32(0.5)) / f32(length)))
    window = (window * np.sqrt(f32(2.0) / np.sum(window * window))).reshape(TAPS, NFFT)
    bins = NFFT // 4 + np.arange(chans)
    phase_index = np.arange(NFFT)[:, None] * bins[None, :] % NFFT
    phases = phase_index.astype(f32) * f32(2.0 * np.pi / NFFT)
    parts = np.stack([np.cos(phases), -np.sin(phases)], 1)
    table = window.T[:, :, None, None] * parts[:, None]
    table = table.reshape(CHUNKS // 2, 2, CHUNK, TAPS * 2 * chans)
    return table.transpose(0, 2, 1, 3).reshape(NFFT // 2, -1).astype(ml_dtypes.bfloat16)


def filter_kernel(
    volts, table, lane_map, flags, out, held, table_v, map_s, flags_s, frames, sums, lanes, rows, in_sem, const_sem
):
    ahead = 3
    arrivals = [
        [
            pltpu.make_async_copy(volts.at[p, :, j], held.at[p, j, pl.ds(0, FRAMES)], in_sem.at[p])
            for j in range(CHUNKS // 2)
        ]
        for p in range(P_DEV)
    ]
    get_table = pltpu.make_async_copy(table, table_v, const_sem.at[0])
    get_map = pltpu.make_async_copy(lane_map, map_s, const_sem.at[1])
    get_flags = pltpu.make_async_copy(flags, flags_s, const_sem.at[2])

    def begin(p):
        for copy in arrivals[p]:
            copy.start()
        if p == 0:
            get_table.start()
        if p == 2:
            get_map.start()
            get_flags.start()

    first_half = lax.broadcasted_iota(jnp.int32, (8, 8, CHUNK), 1) < Q_DEV
    real_lanes = lax.broadcasted_iota(jnp.int32, (CH_DEV, 2 * SPECTRA), 1) < SPECTRA
    lane_group = lax.broadcasted_iota(jnp.int32, (64, CHUNK), 1) // 32

    def pair(low, high):
        upper = first_half[: low.shape[0]]
        straight = jnp.where(upper, low[:, :, :CHUNK], high[:, :, CHUNK:])
        crossed = jnp.where(upper, high[:, :, :CHUNK], low[:, :, CHUNK:])
        return straight + pltpu.roll(crossed, 4, 1)

    def frames_of(p, i, kept):
        spans = [(64 * i, 64), (256 + 64 * i, 64 if i < 3 else 96)]
        block = jnp.concatenate(
            [
                jnp.concatenate([held.at[p, j].reshape(68 * 8, CHUNK)[at : at + size] for at, size in spans], axis=0)
                for j in range(CHUNKS // 2)
            ],
            axis=1,
        )
        both = jnp.dot(block, table_v[...], preferred_element_type=jnp.float32)
        both = both.reshape(-1, 8, 2 * CHUNK)
        frames[p % 2, 8 * i : 8 * i + 8] = pair(both[:8], both[8:16])
        if i == 0:
            return both[8:11]
        if i == 3:
            frames[p % 2, 32:35] = pair(kept, both[16:19])
        return kept

    def taps_of(p, i):
        total = None
        for tap in range(TAPS):
            term = frames[p % 2, 8 * i + tap : 8 * i + tap + 8]
            turn = 32 * (p % 4 - tap) % CHUNK
            if turn:
                term = pltpu.roll(term, turn, 2)
            total = term if total is None else total + term
        total = total.reshape(64, CHUNK)
        at = slice(64 * i, 64 * i + 64)
        sums[p // 4, at] = total if p % 4 == 0 else jnp.where(lane_group == p % 4, total, sums[p // 4, at])

    def finish(first):
        by_q = [
            sums[first // 4, pl.ds(half * Q_DEV + q, SPECTRA // 2, stride=8), :]
            for q in range(Q_DEV)
            for half in range(2)
        ]
        turned = jnp.concatenate(by_q, axis=0).T.reshape(4, 2, CH_DEV, Q_DEV * SPECTRA)
        for i in range(4):
            for q in range(Q_DEV):
                real, imag = (turned[i, part, :, q // 2 * CHUNK : q // 2 * CHUNK + CHUNK] for part in range(2))
                if q % 2:
                    real = pltpu.roll(real, SPECTRA, 1)
                else:
                    imag = pltpu.roll(imag, SPECTRA, 1)
                lanes[(first + i) * Q_DEV + q] = jnp.where(real_lanes, real, imag)

    for p in range(ahead):
        begin(p)
    for p in range(P_DEV):
        for copy in arrivals[p]:
            copy.wait()
        if p + ahead < P_DEV:
            begin(p + ahead)
        if p == 0:
            get_table.wait()
        if p == 5:
            get_map.wait()
            get_flags.wait()
        kept = None
        for i in range(4):
            kept = frames_of(p, i, kept)
            if p > 0:
                taps_of(p - 1, i)
        if p == 5:
            finish(0)
    for i in range(4):
        taps_of(P_DEV - 1, i)
    finish(4)
    for p in range(P_DEV):
        for q in range(Q_DEV):
            weight = flags_s[q, p].astype(jnp.float32)
            rows[pl.ds(q * P_DEV + p, CH_DEV, stride=PITCH), :] = lanes[map_s[0, p * Q_DEV + q]] * weight
    for c in range(CH_DEV):
        out[c] = rows[PITCH * c : PITCH * c + LANES].astype(jnp.bfloat16)


def channelise(voltages, lane_map, input_flags):
    volts = voltages.reshape(P_DEV, Q_DEV, FRAMES, CHUNKS // 2, 2, CHUNK).transpose(0, 2, 3, 4, 1, 5)
    volts = volts.reshape(P_DEV, FRAMES, CHUNKS // 2, 2 * Q_DEV, CHUNK)
    vmem = pl.BlockSpec(memory_space=pltpu.VMEM)
    hbm = pl.BlockSpec(memory_space=pltpu.HBM)
    return pl.pallas_call(
        filter_kernel,
        out_shape=jax.ShapeDtypeStruct((CH_DEV, LANES, 2 * SPECTRA), jnp.bfloat16),
        in_specs=[hbm] * 4,
        out_specs=vmem,
        scratch_shapes=[
            pltpu.VMEM((P_DEV, CHUNKS // 2, 68, 2 * Q_DEV, CHUNK), jnp.bfloat16),
            pltpu.VMEM((NFFT // 2, 2 * CHUNK), jnp.bfloat16),
            pltpu.SMEM((1, LANES), jnp.int32),
            pltpu.SMEM((Q_DEV, P_DEV), jnp.int32),
            pltpu.VMEM((2, 35, 8, CHUNK), jnp.float32),
            pltpu.VMEM((2, 4 * SPECTRA, CHUNK), jnp.float32),
            pltpu.VMEM((LANES, CH_DEV, 2 * SPECTRA), jnp.float32),
            pltpu.VMEM((CH_DEV * PITCH, 2 * SPECTRA), jnp.float32),
            pltpu.SemaphoreType.DMA((P_DEV,)),
            pltpu.SemaphoreType.DMA((3,)),
        ],
        compiler_params=pltpu.CompilerParams(vmem_limit_bytes=50 << 20),
        name="channelise",
    )(
        volts,
        jnp.asarray(filter_table(CH_DEV)),
        lane_map.reshape(1, LANES),
        input_flags.T,
    )


def gather(own):
    def swap(block, d):
        return lax.ppermute(block, "row", [(i, i ^ d) for i in range(ROWS)])

    blocks = {0: own}
    for d in (8, 4, 2, 6):
        blocks[d] = swap(own, d)
    for d in (14, 12, 10):
        blocks[d] = swap(blocks[8], d ^ 8)
    for d in range(0, ROWS, 2):
        blocks[d + 1] = swap(blocks[d], 1)
    late, _ = lax.optimization_barrier((own, blocks[8]))
    other = lax.ppermute(late, "col", [(0, 1), (1, 0)])
    return [blocks[d] for d in range(ROWS)], other


def correlate_kernel(*refs):
    blocks, other = refs[:ROWS], refs[ROWS]
    out, columns, spread, packed, sem = refs[ROWS + 1 :]
    row = lax.axis_index("row")
    first_col = lax.axis_index("col") == 0
    odd = lax.rem(row, 2) == 1
    pair = lax.div(row, 2)
    sign = jnp.where(lax.broadcasted_iota(jnp.int32, (64, 128), 1) < SPECTRA, 1.0, -1.0)
    sign = sign.astype(jnp.bfloat16)
    copies = []
    for c in range(CH_DEV):
        slot = c % 2
        for e in range(ROWS // 2):
            near, far = blocks[2 * e][c], blocks[2 * e + 1][c]
            low, high = jnp.where(odd, far, near), jnp.where(odd, near, far)
            at = pl.multiple_of(lax.bitwise_xor(pair, e) * 16, 16)
            for q in range(Q_DEV):
                both = jnp.concatenate([low[q * 8 : q * 8 + 8], high[q * 8 : q * 8 + 8]], axis=0)
                columns[slot, q, pl.ds(at, 16), :] = both
        mine, theirs = blocks[0][c], other[c]
        left = jnp.concatenate(
            [jnp.where(first_col, mine, theirs), jnp.where(first_col, theirs, mine)], axis=0
        )
        left = jnp.concatenate([left, pltpu.roll(left, SPECTRA, 1) * sign], axis=0)
        for h in range(2):
            right = columns[slot, 2 * h : 2 * h + 2].reshape(256, 2 * SPECTRA)
            products = lax.dot_general(
                left, right, (((1,), (1,)), ((), ())), preferred_element_type=jnp.float32
            ) * (1.0 / SPECTRA)
            for k in range(2):
                for part in range(2):
                    for q in range(2 * Q_DEV):
                        start = (part * 8 + q) * 8
                        spread[slot, part, pl.ds(q * Q_DEV + 2 * h + k, 8, stride=PITCH), :] = products[
                            start : start + 8, k * 128 : k * 128 + 128
                        ]
        for p in range(P_DEV):
            packed[c, :, 32 * p : 32 * p + 32] = spread[slot, :, PITCH * p : PITCH * p + 32].astype(jnp.bfloat16)
        copy = pltpu.make_async_copy(packed.at[c], out.at[c], sem.at[c])
        copy.start()
        copies.append(copy)
    for copy in copies:
        copy.wait()


def correlate(blocks, other):
    vmem = pl.BlockSpec(memory_space=pltpu.VMEM)
    return pl.pallas_call(
        correlate_kernel,
        out_shape=jax.ShapeDtypeStruct((CH_DEV, 2, 2 * LANES * Q_DEV, 8 * ROWS), jnp.bfloat16),
        in_specs=[vmem] * (ROWS + 1),
        out_specs=pl.BlockSpec(memory_space=pltpu.HBM),
        scratch_shapes=[
            pltpu.VMEM((2, Q_DEV, 8 * ROWS, 2 * SPECTRA), jnp.bfloat16),
            pltpu.VMEM((2, 2, P_DEV * PITCH, 8 * ROWS), jnp.float32),
            pltpu.VMEM((CH_DEV, 2, 2 * LANES * Q_DEV, 8 * ROWS), jnp.bfloat16),
            pltpu.SemaphoreType.DMA((CH_DEV,)),
        ],
        compiler_params=pltpu.CompilerParams(vmem_limit_bytes=32 << 20),
        name="correlate",
    )(*blocks, other)


def per_device(voltages, lane_map, input_flags):
    own = channelise(voltages, lane_map, input_flags)
    products = correlate(*gather(own))
    return products.reshape(CH_DEV, 2, P_DEV, 2 * Q_DEV, Q_DEV, P_DEV * ROWS)


def solution(mesh):
    fast = mesh.shape["row"] == ROWS and mesh.shape["col"] == 2 and mesh.shape["chan"] == 1
    return jax.shard_map(
        per_device if fast else per_device_general,
        mesh=mesh,
        in_specs=(P("row", ("col", "chan"), None), P("row", "col", None), P("row", "col")),
        out_specs=P("chan", None, "row", None, "col", None),
        check_vma=False,
    )
```

```python
import jax
import jax.experimental.pallas as pl
import jax.experimental.pallas.tpu as pltpu
import jax.numpy as jnp
import ml_dtypes
import numpy as np
from jax import lax
from jax.sharding import PartitionSpec as P

NFFT = 2048
TAPS = 4
P_DEV = 8
Q_DEV = 4
CH_DEV = 16
SPECTRA = 64
LANES = 32
FRAMES = 67
CHUNK = 128
CHUNKS = NFFT // CHUNK
ROWS = 16


def kernel_table(nfft, taps, chans):
    length = taps * nfft
    position = jnp.arange(length, dtype=jnp.float32)
    centre = (position - length / 2 + 0.5) / nfft
    window = jnp.sinc(centre) * (0.5 - 0.5 * jnp.cos(2.0 * jnp.pi * (position + 0.5) / length))
    norm_scale = jnp.sqrt(2.0 / jnp.sum(window * window))
    window = (window * norm_scale).reshape(taps, nfft)
    sample = jnp.arange(nfft, dtype=jnp.int32)
    bin_index = nfft // 4 + jnp.arange(chans, dtype=jnp.int32)
    phase_index = bin_index[:, None] * sample[None, :] % nfft
    phases = phase_index.astype(jnp.float32) * (2.0 * jnp.pi / nfft)
    both_parts = jnp.stack([jnp.cos(phases).T, -jnp.sin(phases).T], -1)
    built = window.T[:, :, None, None] * both_parts[:, None, :, :]
    return built.reshape(nfft, taps * chans * 2).astype(jnp.bfloat16)


def per_device_general(voltages, lane_map, input_flags):
    all_chans = CH_DEV * lax.axis_size("chan")
    half_q = voltages.shape[1]
    table_rows = kernel_table(NFFT, TAPS, all_chans)
    frames = voltages.reshape(P_DEV, half_q, FRAMES, NFFT)
    frame_sums = jnp.einsum("pqfn,nk->pqfk", frames, table_rows, preferred_element_type=jnp.float32)
    frame_sums = frame_sums.reshape(P_DEV, half_q, FRAMES, TAPS, all_chans, 2)
    tap_sum = frame_sums[:, :, 0:SPECTRA, 0]
    for tap_idx in range(1, TAPS):
        tap_sum = tap_sum + frame_sums[:, :, tap_idx : tap_idx + SPECTRA, tap_idx]
    filtered = tap_sum.astype(jnp.bfloat16)
    filtered = filtered.transpose(3, 0, 1, 4, 2).reshape(all_chans, P_DEV, half_q, 2 * SPECTRA)
    turned_over = lax.all_to_all(filtered, "chan", split_axis=0, concat_axis=2, tiled=True)
    lane_rows = turned_over.reshape(CH_DEV, LANES, 2 * SPECTRA)
    lane_index = lane_map.reshape(LANES)
    selector = (lane_index[:, None] == jnp.arange(LANES, dtype=jnp.int32)[None, :]).astype(
        jnp.bfloat16
    )
    reordered = jnp.einsum("kl,clz->ckz", selector, lane_rows, preferred_element_type=jnp.float32)
    weights = input_flags.reshape(LANES).astype(jnp.float32)[None, :, None]
    channelised = (
        (reordered * weights).astype(jnp.bfloat16).reshape(CH_DEV, P_DEV, Q_DEV, 2 * SPECTRA)
    )
    row_group = lax.all_gather(channelised, "col", axis=2, tiled=True)
    grid_cols = row_group.shape[2]
    row_block = row_group.reshape(CH_DEV, P_DEV * grid_cols, 2 * SPECTRA)
    col_set = lax.all_gather(channelised, "row", axis=1, tiled=True)
    real_part = col_set[..., :SPECTRA]
    imag_part = col_set[..., SPECTRA:]
    turned = jnp.concatenate([-imag_part, real_part], axis=-1)
    col_block = jnp.stack([col_set, turned], axis=1)
    products = jnp.einsum(
        "cik,crpqk->criqp", row_block, col_block, preferred_element_type=jnp.float32
    )
    products = (products * (1.0 / SPECTRA)).astype(jnp.bfloat16)
    return products.reshape(CH_DEV, 2, P_DEV, grid_cols, Q_DEV, col_set.shape[1])


PITCH = 36


def filter_table(chans):
    f32 = np.float32
    length = TAPS * NFFT
    position = np.arange(length, dtype=f32)
    centre = (position - f32(length / 2) + f32(0.5)) / f32(NFFT)
    window = np.sinc(centre.astype(np.float64)).astype(f32)
    window = window * (f32(0.5) - f32(0.5) * np.cos(f32(2.0 * np.pi) * (position + f32(0.5)) / f32(length)))
    window = (window * np.sqrt(f32(2.0) / np.sum(window * window))).reshape(TAPS, NFFT)
    bins = NFFT // 4 + np.arange(chans)
    phase_index = np.arange(NFFT)[:, None] * bins[None, :] % NFFT
    phases = phase_index.astype(f32) * f32(2.0 * np.pi / NFFT)
    parts = np.stack([np.cos(phases), -np.sin(phases)], 1)
    table = window.T[:, :, None, None] * parts[:, None]
    table = table.reshape(CHUNKS // 2, 2, CHUNK, TAPS * 2 * chans)
    return table.transpose(0, 2, 1, 3).reshape(NFFT // 2, -1).astype(ml_dtypes.bfloat16)


def filter_kernel(
    volts, table, lane_map, flags, out, held, table_v, map_s, flags_s, frames, sums, lanes, rows, in_sem, const_sem
):
    ahead = 3
    arrivals = [
        [
            pltpu.make_async_copy(volts.at[p, :, j], held.at[p, j, pl.ds(0, FRAMES)], in_sem.at[p])
            for j in range(CHUNKS // 2)
        ]
        for p in range(P_DEV)
    ]
    get_table = pltpu.make_async_copy(table, table_v, const_sem.at[0])
    get_map = pltpu.make_async_copy(lane_map, map_s, const_sem.at[1])
    get_flags = pltpu.make_async_copy(flags, flags_s, const_sem.at[2])

    def begin(p):
        for copy in arrivals[p]:
            copy.start()
        if p == 0:
            get_table.start()
        if p == 2:
            get_map.start()
            get_flags.start()

    first_half = lax.broadcasted_iota(jnp.int32, (8, 8, CHUNK), 1) < Q_DEV
    real_lanes = lax.broadcasted_iota(jnp.int32, (CH_DEV, 2 * SPECTRA), 1) < SPECTRA
    lane_group = lax.broadcasted_iota(jnp.int32, (64, CHUNK), 1) // 32

    def pair(low, high):
        upper = first_half[: low.shape[0]]
        straight = jnp.where(upper, low[:, :, :CHUNK], high[:, :, CHUNK:])
        crossed = jnp.where(upper, high[:, :, :CHUNK], low[:, :, CHUNK:])
        return straight + pltpu.roll(crossed, 4, 1)

    def frames_of(p, i, kept):
        spans = [(64 * i, 64), (256 + 64 * i, 64 if i < 3 else 96)]
        block = jnp.concatenate(
            [
                jnp.concatenate([held.at[p, j].reshape(68 * 8, CHUNK)[at : at + size] for at, size in spans], axis=0)
                for j in range(CHUNKS // 2)
            ],
            axis=1,
        )
        both = jnp.dot(block, table_v[...], preferred_element_type=jnp.float32)
        both = both.reshape(-1, 8, 2 * CHUNK)
        frames[p % 2, 8 * i : 8 * i + 8] = pair(both[:8], both[8:16])
        if i == 0:
            return both[8:11]
        if i == 3:
            frames[p % 2, 32:35] = pair(kept, both[16:19])
        return kept

    def taps_of(p, i):
        total = None
        for tap in range(TAPS):
            term = frames[p % 2, 8 * i + tap : 8 * i + tap + 8]
            turn = 32 * (p % 4 - tap) % CHUNK
            if turn:
                term = pltpu.roll(term, turn, 2)
            total = term if total is None else total + term
        total = total.reshape(64, CHUNK)
        at = slice(64 * i, 64 * i + 64)
        sums[p // 4, at] = total if p % 4 == 0 else jnp.where(lane_group == p % 4, total, sums[p // 4, at])

    def finish(first):
        by_q = [
            sums[first // 4, pl.ds(half * Q_DEV + q, SPECTRA // 2, stride=8), :]
            for q in range(Q_DEV)
            for half in range(2)
        ]
        turned = jnp.concatenate(by_q, axis=0).T.reshape(4, 2, CH_DEV, Q_DEV * SPECTRA)
        for i in range(4):
            for q in range(Q_DEV):
                real, imag = (turned[i, part, :, q // 2 * CHUNK : q // 2 * CHUNK + CHUNK] for part in range(2))
                if q % 2:
                    real = pltpu.roll(real, SPECTRA, 1)
                else:
                    imag = pltpu.roll(imag, SPECTRA, 1)
                lanes[(first + i) * Q_DEV + q] = jnp.where(real_lanes, real, imag)

    for p in range(ahead):
        begin(p)
    for p in range(P_DEV):
        for copy in arrivals[p]:
            copy.wait()
        if p + ahead < P_DEV:
            begin(p + ahead)
        if p == 0:
            get_table.wait()
        if p == 5:
            get_map.wait()
            get_flags.wait()
        kept = None
        for i in range(4):
            kept = frames_of(p, i, kept)
            if p > 0:
                taps_of(p - 1, i)
        if p == 5:
            finish(0)
    for i in range(4):
        taps_of(P_DEV - 1, i)
    finish(4)
    for p in range(P_DEV):
        for q in range(Q_DEV):
            weight = flags_s[q, p].astype(jnp.float32)
            rows[pl.ds(q * P_DEV + p, CH_DEV, stride=PITCH), :] = lanes[map_s[0, p * Q_DEV + q]] * weight
    for c in range(CH_DEV):
        out[c] = rows[PITCH * c : PITCH * c + LANES].astype(jnp.bfloat16)


def channelise(voltages, lane_map, input_flags):
    volts = voltages.reshape(P_DEV, Q_DEV, FRAMES, CHUNKS // 2, 2, CHUNK).transpose(0, 2, 3, 4, 1, 5)
    volts = volts.reshape(P_DEV, FRAMES, CHUNKS // 2, 2 * Q_DEV, CHUNK)
    vmem = pl.BlockSpec(memory_space=pltpu.VMEM)
    hbm = pl.BlockSpec(memory_space=pltpu.HBM)
    return pl.pallas_call(
        filter_kernel,
        out_shape=jax.ShapeDtypeStruct((CH_DEV, LANES, 2 * SPECTRA), jnp.bfloat16),
        in_specs=[hbm] * 4,
        out_specs=vmem,
        scratch_shapes=[
            pltpu.VMEM((P_DEV, CHUNKS // 2, 68, 2 * Q_DEV, CHUNK), jnp.bfloat16),
            pltpu.VMEM((NFFT // 2, 2 * CHUNK), jnp.bfloat16),
            pltpu.SMEM((1, LANES), jnp.int32),
            pltpu.SMEM((Q_DEV, P_DEV), jnp.int32),
            pltpu.VMEM((2, 35, 8, CHUNK), jnp.float32),
            pltpu.VMEM((2, 4 * SPECTRA, CHUNK), jnp.float32),
            pltpu.VMEM((LANES, CH_DEV, 2 * SPECTRA), jnp.float32),
            pltpu.VMEM((CH_DEV * PITCH, 2 * SPECTRA), jnp.float32),
            pltpu.SemaphoreType.DMA((P_DEV,)),
            pltpu.SemaphoreType.DMA((3,)),
        ],
        compiler_params=pltpu.CompilerParams(vmem_limit_bytes=56 << 20),
        name="channelise",
    )(
        volts,
        jnp.asarray(filter_table(CH_DEV)),
        lane_map.reshape(1, LANES),
        input_flags.T,
    )


def gather(own):
    def swap(block, d):
        return lax.ppermute(block, "row", [(i, i ^ d) for i in range(ROWS)])

    blocks = {0: own}
    for d in (8, 4, 2, 6):
        blocks[d] = swap(own, d)
    for d in (14, 12, 10):
        blocks[d] = swap(blocks[8], d ^ 8)
    for d in range(0, ROWS, 2):
        blocks[d + 1] = swap(blocks[d], 1)
    late, _ = lax.optimization_barrier((own, blocks[8]))
    other = lax.ppermute(late, "col", [(0, 1), (1, 0)])
    blocks[0] = swap(blocks[1], 1)
    return [blocks[d] for d in range(ROWS)], other


def correlate_kernel(*refs):
    blocks, other = refs[:ROWS], refs[ROWS]
    out, columns, spread, packed, sem = refs[ROWS + 1 :]
    row = lax.axis_index("row")
    first_col = lax.axis_index("col") == 0
    odd = lax.rem(row, 2) == 1
    pair = lax.div(row, 2)
    sign = jnp.where(lax.broadcasted_iota(jnp.int32, (64, 128), 1) < SPECTRA, 1.0, -1.0)
    sign = sign.astype(jnp.bfloat16)
    copies = []
    for c in range(CH_DEV):
        slot = c % 2
        for e in range(ROWS // 2):
            near, far = blocks[2 * e][c], blocks[2 * e + 1][c]
            low, high = jnp.where(odd, far, near), jnp.where(odd, near, far)
            at = pl.multiple_of(lax.bitwise_xor(pair, e) * 16, 16)
            for q in range(Q_DEV):
                both = jnp.concatenate([low[q * 8 : q * 8 + 8], high[q * 8 : q * 8 + 8]], axis=0)
                columns[slot, q, pl.ds(at, 16), :] = both
        mine, theirs = blocks[0][c], other[c]
        left = jnp.concatenate(
            [jnp.where(first_col, mine, theirs), jnp.where(first_col, theirs, mine)], axis=0
        )
        left = jnp.concatenate([left, pltpu.roll(left, SPECTRA, 1) * sign], axis=0)
        for h in range(2):
            right = columns[slot, 2 * h : 2 * h + 2].reshape(256, 2 * SPECTRA)
            products = lax.dot_general(
                left, right, (((1,), (1,)), ((), ())), preferred_element_type=jnp.float32
            ) * (1.0 / SPECTRA)
            for k in range(2):
                for part in range(2):
                    for q in range(2 * Q_DEV):
                        start = (part * 8 + q) * 8
                        spread[slot, part, pl.ds(q * Q_DEV + 2 * h + k, 8, stride=PITCH), :] = products[
                            start : start + 8, k * 128 : k * 128 + 128
                        ]
        for p in range(P_DEV):
            packed[c, :, 32 * p : 32 * p + 32] = spread[slot, :, PITCH * p : PITCH * p + 32].astype(jnp.bfloat16)
        copy = pltpu.make_async_copy(packed.at[c], out.at[c], sem.at[c])
        copy.start()
        copies.append(copy)
    for copy in copies:
        copy.wait()


def correlate(blocks, other):
    vmem = pl.BlockSpec(memory_space=pltpu.VMEM)
    return pl.pallas_call(
        correlate_kernel,
        out_shape=jax.ShapeDtypeStruct((CH_DEV, 2, 2 * LANES * Q_DEV, 8 * ROWS), jnp.bfloat16),
        in_specs=[vmem] * (ROWS + 1),
        out_specs=pl.BlockSpec(memory_space=pltpu.HBM),
        scratch_shapes=[
            pltpu.VMEM((2, Q_DEV, 8 * ROWS, 2 * SPECTRA), jnp.bfloat16),
            pltpu.VMEM((2, 2, P_DEV * PITCH, 8 * ROWS), jnp.float32),
            pltpu.VMEM((CH_DEV, 2, 2 * LANES * Q_DEV, 8 * ROWS), jnp.bfloat16),
            pltpu.SemaphoreType.DMA((CH_DEV,)),
        ],
        compiler_params=pltpu.CompilerParams(vmem_limit_bytes=32 << 20),
        name="correlate",
    )(*blocks, other)


def per_device(voltages, lane_map, input_flags):
    own = channelise(voltages, lane_map, input_flags)
    products = correlate(*gather(own))
    return products.reshape(CH_DEV, 2, P_DEV, 2 * Q_DEV, Q_DEV, P_DEV * ROWS)


def solution(mesh):
    fast = mesh.shape["row"] == ROWS and mesh.shape["col"] == 2 and mesh.shape["chan"] == 1
    return jax.shard_map(
        per_device if fast else per_device_general,
        mesh=mesh,
        in_specs=(P("row", ("col", "chan"), None), P("row", "col", None), P("row", "col")),
        out_specs=P("chan", None, "row", None, "col", None),
        check_vma=False,
    )
```

```python
import jax
import jax.experimental.pallas as pl
import jax.experimental.pallas.tpu as pltpu
import jax.numpy as jnp
import ml_dtypes
import numpy as np
from jax import lax
from jax.sharding import PartitionSpec as P

NFFT = 2048
TAPS = 4
P_DEV = 8
Q_DEV = 4
CH_DEV = 16
SPECTRA = 64
LANES = 32
FRAMES = 67
CHUNK = 128
CHUNKS = NFFT // CHUNK
ROWS = 16


def kernel_table(nfft, taps, chans):
    length = taps * nfft
    position = jnp.arange(length, dtype=jnp.float32)
    centre = (position - length / 2 + 0.5) / nfft
    window = jnp.sinc(centre) * (0.5 - 0.5 * jnp.cos(2.0 * jnp.pi * (position + 0.5) / length))
    norm_scale = jnp.sqrt(2.0 / jnp.sum(window * window))
    window = (window * norm_scale).reshape(taps, nfft)
    sample = jnp.arange(nfft, dtype=jnp.int32)
    bin_index = nfft // 4 + jnp.arange(chans, dtype=jnp.int32)
    phase_index = bin_index[:, None] * sample[None, :] % nfft
    phases = phase_index.astype(jnp.float32) * (2.0 * jnp.pi / nfft)
    both_parts = jnp.stack([jnp.cos(phases).T, -jnp.sin(phases).T], -1)
    built = window.T[:, :, None, None] * both_parts[:, None, :, :]
    return built.reshape(nfft, taps * chans * 2).astype(jnp.bfloat16)


def per_device_general(voltages, lane_map, input_flags):
    all_chans = CH_DEV * lax.axis_size("chan")
    half_q = voltages.shape[1]
    table_rows = kernel_table(NFFT, TAPS, all_chans)
    frames = voltages.reshape(P_DEV, half_q, FRAMES, NFFT)
    frame_sums = jnp.einsum("pqfn,nk->pqfk", frames, table_rows, preferred_element_type=jnp.float32)
    frame_sums = frame_sums.reshape(P_DEV, half_q, FRAMES, TAPS, all_chans, 2)
    tap_sum = frame_sums[:, :, 0:SPECTRA, 0]
    for tap_idx in range(1, TAPS):
        tap_sum = tap_sum + frame_sums[:, :, tap_idx : tap_idx + SPECTRA, tap_idx]
    filtered = tap_sum.astype(jnp.bfloat16)
    filtered = filtered.transpose(3, 0, 1, 4, 2).reshape(all_chans, P_DEV, half_q, 2 * SPECTRA)
    turned_over = lax.all_to_all(filtered, "chan", split_axis=0, concat_axis=2, tiled=True)
    lane_rows = turned_over.reshape(CH_DEV, LANES, 2 * SPECTRA)
    lane_index = lane_map.reshape(LANES)
    selector = (lane_index[:, None] == jnp.arange(LANES, dtype=jnp.int32)[None, :]).astype(
        jnp.bfloat16
    )
    reordered = jnp.einsum("kl,clz->ckz", selector, lane_rows, preferred_element_type=jnp.float32)
    weights = input_flags.reshape(LANES).astype(jnp.float32)[None, :, None]
    channelised = (
        (reordered * weights).astype(jnp.bfloat16).reshape(CH_DEV, P_DEV, Q_DEV, 2 * SPECTRA)
    )
    row_group = lax.all_gather(channelised, "col", axis=2, tiled=True)
    grid_cols = row_group.shape[2]
    row_block = row_group.reshape(CH_DEV, P_DEV * grid_cols, 2 * SPECTRA)
    col_set = lax.all_gather(channelised, "row", axis=1, tiled=True)
    real_part = col_set[..., :SPECTRA]
    imag_part = col_set[..., SPECTRA:]
    turned = jnp.concatenate([-imag_part, real_part], axis=-1)
    col_block = jnp.stack([col_set, turned], axis=1)
    products = jnp.einsum(
        "cik,crpqk->criqp", row_block, col_block, preferred_element_type=jnp.float32
    )
    products = (products * (1.0 / SPECTRA)).astype(jnp.bfloat16)
    return products.reshape(CH_DEV, 2, P_DEV, grid_cols, Q_DEV, col_set.shape[1])


PITCH = 36


def filter_table(chans):
    f32 = np.float32
    length = TAPS * NFFT
    position = np.arange(length, dtype=f32)
    centre = (position - f32(length / 2) + f32(0.5)) / f32(NFFT)
    window = np.sinc(centre.astype(np.float64)).astype(f32)
    window = window * (f32(0.5) - f32(0.5) * np.cos(f32(2.0 * np.pi) * (position + f32(0.5)) / f32(length)))
    window = (window * np.sqrt(f32(2.0) / np.sum(window * window))).reshape(TAPS, NFFT)
    bins = NFFT // 4 + np.arange(chans)
    phase_index = np.arange(NFFT)[:, None] * bins[None, :] % NFFT
    phases = phase_index.astype(f32) * f32(2.0 * np.pi / NFFT)
    parts = np.stack([np.cos(phases), -np.sin(phases)], 1)
    table = window.T[:, :, None, None] * parts[:, None]
    table = table.reshape(CHUNKS // 2, 2, CHUNK, TAPS * 2 * chans)
    return table.transpose(0, 2, 1, 3).reshape(NFFT // 2, -1).astype(ml_dtypes.bfloat16)


def filter_kernel(
    volts, table, lane_map, flags, out, held, table_v, map_s, flags_s, frames, sums, lanes, rows, in_sem, const_sem
):
    spans = ((0, 2), (2, 5), (5, 8))
    arrivals = [
        [
            pltpu.make_async_copy(
                volts.at[pl.ds(low, high - low), :, j],
                held.at[pl.ds(low, high - low), j, pl.ds(0, FRAMES)],
                in_sem.at[k],
            )
            for j in range(CHUNKS // 2)
        ]
        for k, (low, high) in enumerate(spans)
    ]
    get_table = pltpu.make_async_copy(table, table_v, const_sem.at[0])
    get_map = pltpu.make_async_copy(lane_map, map_s, const_sem.at[1])
    get_flags = pltpu.make_async_copy(flags, flags_s, const_sem.at[2])

    def begin(k):
        for copy in arrivals[k]:
            copy.start()
        if k == 0:
            get_table.start()
        if k == 1:
            get_map.start()
            get_flags.start()

    first_half = lax.broadcasted_iota(jnp.int32, (8, 8, CHUNK), 1) < Q_DEV
    real_lanes = lax.broadcasted_iota(jnp.int32, (CH_DEV, 2 * SPECTRA), 1) < SPECTRA
    lane_group = lax.broadcasted_iota(jnp.int32, (64, CHUNK), 1) // 32

    def pair(low, high):
        upper = first_half[: low.shape[0]]
        straight = jnp.where(upper, low[:, :, :CHUNK], high[:, :, CHUNK:])
        crossed = jnp.where(upper, high[:, :, :CHUNK], low[:, :, CHUNK:])
        return straight + pltpu.roll(crossed, 4, 1)

    def frames_of(p, i, kept):
        spans = [(64 * i, 64), (256 + 64 * i, 64 if i < 3 else 96)]
        block = jnp.concatenate(
            [
                jnp.concatenate([held.at[p, j].reshape(68 * 8, CHUNK)[at : at + size] for at, size in spans], axis=0)
                for j in range(CHUNKS // 2)
            ],
            axis=1,
        )
        both = jnp.dot(block, table_v[...], preferred_element_type=jnp.float32)
        both = both.reshape(-1, 8, 2 * CHUNK)
        frames[p % 2, 8 * i : 8 * i + 8] = pair(both[:8], both[8:16])
        if i == 0:
            return both[8:11]
        if i == 3:
            frames[p % 2, 32:35] = pair(kept, both[16:19])
        return kept

    def taps_of(p, i):
        total = None
        for tap in range(TAPS):
            term = frames[p % 2, 8 * i + tap : 8 * i + tap + 8]
            turn = 32 * (p % 4 - tap) % CHUNK
            if turn:
                term = pltpu.roll(term, turn, 2)
            total = term if total is None else total + term
        total = total.reshape(64, CHUNK)
        at = slice(64 * i, 64 * i + 64)
        sums[p // 4, at] = total if p % 4 == 0 else jnp.where(lane_group == p % 4, total, sums[p // 4, at])

    def finish(first):
        by_q = [
            sums[first // 4, pl.ds(half * Q_DEV + q, SPECTRA // 2, stride=8), :]
            for q in range(Q_DEV)
            for half in range(2)
        ]
        turned = jnp.concatenate(by_q, axis=0).T.reshape(4, 2, CH_DEV, Q_DEV * SPECTRA)
        for i in range(4):
            for q in range(Q_DEV):
                real, imag = (turned[i, part, :, q // 2 * CHUNK : q // 2 * CHUNK + CHUNK] for part in range(2))
                if q % 2:
                    real = pltpu.roll(real, SPECTRA, 1)
                else:
                    imag = pltpu.roll(imag, SPECTRA, 1)
                lanes[(first + i) * Q_DEV + q] = jnp.where(real_lanes, real, imag)

    for k in range(len(spans)):
        begin(k)
    for p in range(P_DEV):
        for k, (low, _) in enumerate(spans):
            if p == low:
                for copy in arrivals[k]:
                    copy.wait()
        if p == 0:
            get_table.wait()
        if p == 5:
            get_map.wait()
            get_flags.wait()
        kept = None
        for i in range(4):
            kept = frames_of(p, i, kept)
            if p > 0:
                taps_of(p - 1, i)
        if p == 5:
            finish(0)
    for i in range(4):
        taps_of(P_DEV - 1, i)
    finish(4)
    for p in range(P_DEV):
        for q in range(Q_DEV):
            weight = flags_s[q, p].astype(jnp.float32)
            rows[pl.ds(q * P_DEV + p, CH_DEV, stride=PITCH), :] = lanes[map_s[0, p * Q_DEV + q]] * weight
    for c in range(CH_DEV):
        out[c] = rows[PITCH * c : PITCH * c + LANES].astype(jnp.bfloat16)


def channelise(voltages, lane_map, input_flags):
    volts = voltages.reshape(P_DEV, Q_DEV, FRAMES, CHUNKS // 2, 2, CHUNK).transpose(0, 2, 3, 4, 1, 5)
    volts = volts.reshape(P_DEV, FRAMES, CHUNKS // 2, 2 * Q_DEV, CHUNK)
    vmem = pl.BlockSpec(memory_space=pltpu.VMEM)
    hbm = pl.BlockSpec(memory_space=pltpu.HBM)
    return pl.pallas_call(
        filter_kernel,
        out_shape=jax.ShapeDtypeStruct((CH_DEV, LANES, 2 * SPECTRA), jnp.bfloat16),
        in_specs=[hbm] * 4,
        out_specs=vmem,
        scratch_shapes=[
            pltpu.VMEM((P_DEV, CHUNKS // 2, 68, 2 * Q_DEV, CHUNK), jnp.bfloat16),
            pltpu.VMEM((NFFT // 2, 2 * CHUNK), jnp.bfloat16),
            pltpu.SMEM((1, LANES), jnp.int32),
            pltpu.SMEM((Q_DEV, P_DEV), jnp.int32),
            pltpu.VMEM((2, 35, 8, CHUNK), jnp.float32),
            pltpu.VMEM((2, 4 * SPECTRA, CHUNK), jnp.float32),
            pltpu.VMEM((LANES, CH_DEV, 2 * SPECTRA), jnp.float32),
            pltpu.VMEM((CH_DEV * PITCH, 2 * SPECTRA), jnp.float32),
            pltpu.SemaphoreType.DMA((3,)),
            pltpu.SemaphoreType.DMA((3,)),
        ],
        compiler_params=pltpu.CompilerParams(vmem_limit_bytes=56 << 20),
        name="channelise",
    )(
        volts,
        jnp.asarray(filter_table(CH_DEV)),
        lane_map.reshape(1, LANES),
        input_flags.T,
    )


def gather(own):
    def swap(block, d):
        return lax.ppermute(block, "row", [(i, i ^ d) for i in range(ROWS)])

    blocks = {0: own}
    for d in (8, 4, 2, 6):
        blocks[d] = swap(own, d)
    for d in (14, 12, 10):
        blocks[d] = swap(blocks[8], d ^ 8)
    for d in range(0, ROWS, 2):
        blocks[d + 1] = swap(blocks[d], 1)
    late, _ = lax.optimization_barrier((own, blocks[8]))
    other = lax.ppermute(late, "col", [(0, 1), (1, 0)])
    blocks[0] = swap(blocks[1], 1)
    return [blocks[d] for d in range(ROWS)], other


def correlate_kernel(*refs):
    blocks, other = refs[:ROWS], refs[ROWS]
    out, columns, spread, packed, sem = refs[ROWS + 1 :]
    row = lax.axis_index("row")
    first_col = lax.axis_index("col") == 0
    odd = lax.rem(row, 2) == 1
    pair = lax.div(row, 2)
    sign = jnp.where(lax.broadcasted_iota(jnp.int32, (64, 128), 1) < SPECTRA, 1.0, -1.0)
    sign = sign.astype(jnp.bfloat16)
    copies = []
    for c in range(CH_DEV):
        slot = c % 2
        for e in range(ROWS // 2):
            near, far = blocks[2 * e][c], blocks[2 * e + 1][c]
            low, high = jnp.where(odd, far, near), jnp.where(odd, near, far)
            at = pl.multiple_of(lax.bitwise_xor(pair, e) * 16, 16)
            for q in range(Q_DEV):
                both = jnp.concatenate([low[q * 8 : q * 8 + 8], high[q * 8 : q * 8 + 8]], axis=0)
                columns[slot, q, pl.ds(at, 16), :] = both
        mine, theirs = blocks[0][c], other[c]
        left = jnp.concatenate(
            [jnp.where(first_col, mine, theirs), jnp.where(first_col, theirs, mine)], axis=0
        )
        left = jnp.concatenate([left, pltpu.roll(left, SPECTRA, 1) * sign], axis=0)
        for h in range(2):
            right = columns[slot, 2 * h : 2 * h + 2].reshape(256, 2 * SPECTRA)
            products = lax.dot_general(
                left, right, (((1,), (1,)), ((), ())), preferred_element_type=jnp.float32
            ) * (1.0 / SPECTRA)
            for k in range(2):
                for part in range(2):
                    for q in range(2 * Q_DEV):
                        start = (part * 8 + q) * 8
                        spread[slot, part, pl.ds(q * Q_DEV + 2 * h + k, 8, stride=PITCH), :] = products[
                            start : start + 8, k * 128 : k * 128 + 128
                        ]
        for p in range(P_DEV):
            packed[c, :, 32 * p : 32 * p + 32] = spread[slot, :, PITCH * p : PITCH * p + 32].astype(jnp.bfloat16)
        copy = pltpu.make_async_copy(packed.at[c], out.at[c], sem.at[c])
        copy.start()
        copies.append(copy)
    for copy in copies:
        copy.wait()


def correlate(blocks, other):
    vmem = pl.BlockSpec(memory_space=pltpu.VMEM)
    return pl.pallas_call(
        correlate_kernel,
        out_shape=jax.ShapeDtypeStruct((CH_DEV, 2, 2 * LANES * Q_DEV, 8 * ROWS), jnp.bfloat16),
        in_specs=[vmem] * (ROWS + 1),
        out_specs=pl.BlockSpec(memory_space=pltpu.HBM),
        scratch_shapes=[
            pltpu.VMEM((2, Q_DEV, 8 * ROWS, 2 * SPECTRA), jnp.bfloat16),
            pltpu.VMEM((2, 2, P_DEV * PITCH, 8 * ROWS), jnp.float32),
            pltpu.VMEM((CH_DEV, 2, 2 * LANES * Q_DEV, 8 * ROWS), jnp.bfloat16),
            pltpu.SemaphoreType.DMA((CH_DEV,)),
        ],
        compiler_params=pltpu.CompilerParams(vmem_limit_bytes=32 << 20),
        name="correlate",
    )(*blocks, other)


def per_device(voltages, lane_map, input_flags):
    own = channelise(voltages, lane_map, input_flags)
    products = correlate(*gather(own))
    return products.reshape(CH_DEV, 2, P_DEV, 2 * Q_DEV, Q_DEV, P_DEV * ROWS)


def solution(mesh):
    fast = mesh.shape["row"] == ROWS and mesh.shape["col"] == 2 and mesh.shape["chan"] == 1
    return jax.shard_map(
        per_device if fast else per_device_general,
        mesh=mesh,
        in_specs=(P("row", ("col", "chan"), None), P("row", "col", None), P("row", "col")),
        out_specs=P("chan", None, "row", None, "col", None),
        check_vma=False,
    )
```

```python
import jax
import jax.experimental.pallas as pl
import jax.experimental.pallas.tpu as pltpu
import jax.numpy as jnp
import ml_dtypes
import numpy as np
from jax import lax
from jax.sharding import PartitionSpec as P

NFFT = 2048
TAPS = 4
P_DEV = 8
Q_DEV = 4
CH_DEV = 16
SPECTRA = 64
LANES = 32
FRAMES = 67
CHUNK = 128
CHUNKS = NFFT // CHUNK
ROWS = 16


def kernel_table(nfft, taps, chans):
    length = taps * nfft
    position = jnp.arange(length, dtype=jnp.float32)
    centre = (position - length / 2 + 0.5) / nfft
    window = jnp.sinc(centre) * (0.5 - 0.5 * jnp.cos(2.0 * jnp.pi * (position + 0.5) / length))
    norm_scale = jnp.sqrt(2.0 / jnp.sum(window * window))
    window = (window * norm_scale).reshape(taps, nfft)
    sample = jnp.arange(nfft, dtype=jnp.int32)
    bin_index = nfft // 4 + jnp.arange(chans, dtype=jnp.int32)
    phase_index = bin_index[:, None] * sample[None, :] % nfft
    phases = phase_index.astype(jnp.float32) * (2.0 * jnp.pi / nfft)
    both_parts = jnp.stack([jnp.cos(phases).T, -jnp.sin(phases).T], -1)
    built = window.T[:, :, None, None] * both_parts[:, None, :, :]
    return built.reshape(nfft, taps * chans * 2).astype(jnp.bfloat16)


def per_device_general(voltages, lane_map, input_flags):
    all_chans = CH_DEV * lax.axis_size("chan")
    half_q = voltages.shape[1]
    table_rows = kernel_table(NFFT, TAPS, all_chans)
    frames = voltages.reshape(P_DEV, half_q, FRAMES, NFFT)
    frame_sums = jnp.einsum("pqfn,nk->pqfk", frames, table_rows, preferred_element_type=jnp.float32)
    frame_sums = frame_sums.reshape(P_DEV, half_q, FRAMES, TAPS, all_chans, 2)
    tap_sum = frame_sums[:, :, 0:SPECTRA, 0]
    for tap_idx in range(1, TAPS):
        tap_sum = tap_sum + frame_sums[:, :, tap_idx : tap_idx + SPECTRA, tap_idx]
    filtered = tap_sum.astype(jnp.bfloat16)
    filtered = filtered.transpose(3, 0, 1, 4, 2).reshape(all_chans, P_DEV, half_q, 2 * SPECTRA)
    turned_over = lax.all_to_all(filtered, "chan", split_axis=0, concat_axis=2, tiled=True)
    lane_rows = turned_over.reshape(CH_DEV, LANES, 2 * SPECTRA)
    lane_index = lane_map.reshape(LANES)
    selector = (lane_index[:, None] == jnp.arange(LANES, dtype=jnp.int32)[None, :]).astype(
        jnp.bfloat16
    )
    reordered = jnp.einsum("kl,clz->ckz", selector, lane_rows, preferred_element_type=jnp.float32)
    weights = input_flags.reshape(LANES).astype(jnp.float32)[None, :, None]
    channelised = (
        (reordered * weights).astype(jnp.bfloat16).reshape(CH_DEV, P_DEV, Q_DEV, 2 * SPECTRA)
    )
    row_group = lax.all_gather(channelised, "col", axis=2, tiled=True)
    grid_cols = row_group.shape[2]
    row_block = row_group.reshape(CH_DEV, P_DEV * grid_cols, 2 * SPECTRA)
    col_set = lax.all_gather(channelised, "row", axis=1, tiled=True)
    real_part = col_set[..., :SPECTRA]
    imag_part = col_set[..., SPECTRA:]
    turned = jnp.concatenate([-imag_part, real_part], axis=-1)
    col_block = jnp.stack([col_set, turned], axis=1)
    products = jnp.einsum(
        "cik,crpqk->criqp", row_block, col_block, preferred_element_type=jnp.float32
    )
    products = (products * (1.0 / SPECTRA)).astype(jnp.bfloat16)
    return products.reshape(CH_DEV, 2, P_DEV, grid_cols, Q_DEV, col_set.shape[1])


PITCH = 36


def filter_table(chans):
    f32 = np.float32
    length = TAPS * NFFT
    position = np.arange(length, dtype=f32)
    centre = (position - f32(length / 2) + f32(0.5)) / f32(NFFT)
    window = np.sinc(centre.astype(np.float64)).astype(f32)
    window = window * (f32(0.5) - f32(0.5) * np.cos(f32(2.0 * np.pi) * (position + f32(0.5)) / f32(length)))
    window = (window * np.sqrt(f32(2.0) / np.sum(window * window))).reshape(TAPS, NFFT)
    bins = NFFT // 4 + np.arange(chans)
    phase_index = np.arange(NFFT)[:, None] * bins[None, :] % NFFT
    phases = phase_index.astype(f32) * f32(2.0 * np.pi / NFFT)
    parts = np.stack([np.cos(phases), -np.sin(phases)], 1)
    table = window.T[:, :, None, None] * parts[:, None]
    table = table.reshape(CHUNKS // 2, 2, CHUNK, TAPS * 2 * chans)
    return table.transpose(0, 2, 1, 3).reshape(NFFT // 2, -1).astype(ml_dtypes.bfloat16)


def filter_kernel(
    volts, table, lane_map, flags, out, held, table_v, map_s, flags_s, frames, sums, lanes, rows, in_sem, const_sem
):
    spans = ((0, 2), (2, 5), (5, 8))
    arrivals = [
        [
            pltpu.make_async_copy(
                volts.at[pl.ds(low, high - low), :, j],
                held.at[pl.ds(low, high - low), j, pl.ds(0, FRAMES)],
                in_sem.at[k],
            )
            for j in range(CHUNKS // 2)
        ]
        for k, (low, high) in enumerate(spans)
    ]
    get_table = pltpu.make_async_copy(table, table_v, const_sem.at[0])
    get_map = pltpu.make_async_copy(lane_map, map_s, const_sem.at[1])
    get_flags = pltpu.make_async_copy(flags, flags_s, const_sem.at[2])

    def begin(k):
        for copy in arrivals[k]:
            copy.start()
        if k == 0:
            get_table.start()
        if k == 1:
            get_map.start()
            get_flags.start()

    first_half = lax.broadcasted_iota(jnp.int32, (8, 8, CHUNK), 1) < Q_DEV
    real_lanes = lax.broadcasted_iota(jnp.int32, (CH_DEV, 2 * SPECTRA), 1) < SPECTRA
    lane_group = lax.broadcasted_iota(jnp.int32, (64, CHUNK), 1) // 32

    def pair(low, high):
        upper = first_half[: low.shape[0]]
        straight = jnp.where(upper, low[:, :, :CHUNK], high[:, :, CHUNK:])
        crossed = jnp.where(upper, high[:, :, :CHUNK], low[:, :, CHUNK:])
        return straight + pltpu.roll(crossed, 4, 1)

    def frames_of(p, i, kept):
        spans = [(64 * i, 64), (256 + 64 * i, 64 if i < 3 else 96)]
        block = jnp.concatenate(
            [
                jnp.concatenate([held.at[p, j].reshape(68 * 8, CHUNK)[at : at + size] for at, size in spans], axis=0)
                for j in range(CHUNKS // 2)
            ],
            axis=1,
        )
        both = jnp.dot(block, table_v[...], preferred_element_type=jnp.float32)
        both = both.reshape(-1, 8, 2 * CHUNK)
        frames[p % 2, 8 * i : 8 * i + 8] = pair(both[:8], both[8:16])
        if i == 0:
            return both[8:11]
        if i == 3:
            frames[p % 2, 32:35] = pair(kept, both[16:19])
        return kept

    def taps_of(p, i):
        total = None
        for tap in range(TAPS):
            term = frames[p % 2, 8 * i + tap : 8 * i + tap + 8]
            turn = 32 * (p % 4 - tap) % CHUNK
            if turn:
                term = pltpu.roll(term, turn, 2)
            total = term if total is None else total + term
        total = total.reshape(64, CHUNK)
        at = slice(64 * i, 64 * i + 64)
        sums[p // 4, at] = total if p % 4 == 0 else jnp.where(lane_group == p % 4, total, sums[p // 4, at])

    def finish(first):
        by_q = [
            sums[first // 4, pl.ds(half * Q_DEV + q, SPECTRA // 2, stride=8), :]
            for q in range(Q_DEV)
            for half in range(2)
        ]
        turned = jnp.concatenate(by_q, axis=0).T.reshape(4, 2, CH_DEV, Q_DEV * SPECTRA)
        for i in range(4):
            for q in range(Q_DEV):
                real, imag = (turned[i, part, :, q // 2 * CHUNK : q // 2 * CHUNK + CHUNK] for part in range(2))
                if q % 2:
                    real = pltpu.roll(real, SPECTRA, 1)
                else:
                    imag = pltpu.roll(imag, SPECTRA, 1)
                lanes[(first + i) * Q_DEV + q] = jnp.where(real_lanes, real, imag)

    for k in range(len(spans)):
        begin(k)
    for p in range(P_DEV):
        for k, (low, _) in enumerate(spans):
            if p == low:
                for copy in arrivals[k]:
                    copy.wait()
        if p == 0:
            get_table.wait()
        if p == 5:
            get_map.wait()
            get_flags.wait()
        kept = None
        for i in range(4):
            kept = frames_of(p, i, kept)
            if p > 0:
                taps_of(p - 1, i)
        if p == 5:
            finish(0)
    for i in range(4):
        taps_of(P_DEV - 1, i)
    finish(4)
    for p in range(P_DEV):
        for q in range(Q_DEV):
            weight = flags_s[q, p].astype(jnp.float32)
            rows[pl.ds(q * P_DEV + p, CH_DEV, stride=PITCH), :] = lanes[map_s[0, p * Q_DEV + q]] * weight
    for c in range(CH_DEV):
        out[c] = rows[PITCH * c : PITCH * c + LANES].astype(jnp.bfloat16)


def channelise(voltages, lane_map, input_flags):
    volts = voltages.reshape(P_DEV, Q_DEV, FRAMES, CHUNKS // 2, 2, CHUNK).transpose(0, 2, 3, 4, 1, 5)
    volts = volts.reshape(P_DEV, FRAMES, CHUNKS // 2, 2 * Q_DEV, CHUNK)
    vmem = pl.BlockSpec(memory_space=pltpu.VMEM)
    hbm = pl.BlockSpec(memory_space=pltpu.HBM)
    return pl.pallas_call(
        filter_kernel,
        out_shape=jax.ShapeDtypeStruct((CH_DEV, LANES, 2 * SPECTRA), jnp.bfloat16),
        in_specs=[hbm] * 4,
        out_specs=vmem,
        scratch_shapes=[
            pltpu.VMEM((P_DEV, CHUNKS // 2, 68, 2 * Q_DEV, CHUNK), jnp.bfloat16),
            pltpu.VMEM((NFFT // 2, 2 * CHUNK), jnp.bfloat16),
            pltpu.SMEM((1, LANES), jnp.int32),
            pltpu.SMEM((Q_DEV, P_DEV), jnp.int32),
            pltpu.VMEM((2, 35, 8, CHUNK), jnp.float32),
            pltpu.VMEM((2, 4 * SPECTRA, CHUNK), jnp.float32),
            pltpu.VMEM((LANES, CH_DEV, 2 * SPECTRA), jnp.float32),
            pltpu.VMEM((CH_DEV * PITCH, 2 * SPECTRA), jnp.float32),
            pltpu.SemaphoreType.DMA((3,)),
            pltpu.SemaphoreType.DMA((3,)),
        ],
        compiler_params=pltpu.CompilerParams(vmem_limit_bytes=56 << 20),
        name="channelise",
    )(
        volts,
        jnp.asarray(filter_table(CH_DEV)),
        lane_map.reshape(1, LANES),
        input_flags.T,
    )


def gather(own):
    def swap(block, d):
        return lax.ppermute(block, "row", [(i, i ^ d) for i in range(ROWS)])

    blocks = {0: own}
    for d in (8, 4, 2, 6):
        blocks[d] = swap(own, d)
    for d in (14, 12, 10):
        blocks[d] = swap(blocks[8], d ^ 8)
    for d in range(0, ROWS, 2):
        blocks[d + 1] = swap(blocks[d], 1)
    late, _ = lax.optimization_barrier((own, blocks[8]))
    other = lax.ppermute(late, "col", [(0, 1), (1, 0)])
    back, _ = lax.optimization_barrier((blocks[1], blocks[6]))
    blocks[0] = swap(back, 1)
    return [blocks[d] for d in range(ROWS)], other


def correlate_kernel(*refs):
    blocks, other = refs[:ROWS], refs[ROWS]
    out, columns, spread, packed, sem = refs[ROWS + 1 :]
    row = lax.axis_index("row")
    first_col = lax.axis_index("col") == 0
    odd = lax.rem(row, 2) == 1
    pair = lax.div(row, 2)
    sign = jnp.where(lax.broadcasted_iota(jnp.int32, (64, 128), 1) < SPECTRA, 1.0, -1.0)
    sign = sign.astype(jnp.bfloat16)
    copies = []
    for c in range(CH_DEV):
        slot = c % 2
        for e in range(ROWS // 2):
            near, far = blocks[2 * e][c], blocks[2 * e + 1][c]
            low, high = jnp.where(odd, far, near), jnp.where(odd, near, far)
            at = pl.multiple_of(lax.bitwise_xor(pair, e) * 16, 16)
            for q in range(Q_DEV):
                both = jnp.concatenate([low[q * 8 : q * 8 + 8], high[q * 8 : q * 8 + 8]], axis=0)
                columns[slot, q, pl.ds(at, 16), :] = both
        mine, theirs = blocks[0][c], other[c]
        left = jnp.concatenate(
            [jnp.where(first_col, mine, theirs), jnp.where(first_col, theirs, mine)], axis=0
        )
        left = jnp.concatenate([left, pltpu.roll(left, SPECTRA, 1) * sign], axis=0)
        for h in range(2):
            right = columns[slot, 2 * h : 2 * h + 2].reshape(256, 2 * SPECTRA)
            products = lax.dot_general(
                left, right, (((1,), (1,)), ((), ())), preferred_element_type=jnp.float32
            ) * (1.0 / SPECTRA)
            for k in range(2):
                for part in range(2):
                    for q in range(2 * Q_DEV):
                        start = (part * 8 + q) * 8
                        spread[slot, part, pl.ds(q * Q_DEV + 2 * h + k, 8, stride=PITCH), :] = products[
                            start : start + 8, k * 128 : k * 128 + 128
                        ]
        for p in range(P_DEV):
            packed[c, :, 32 * p : 32 * p + 32] = spread[slot, :, PITCH * p : PITCH * p + 32].astype(jnp.bfloat16)
        copy = pltpu.make_async_copy(packed.at[c], out.at[c], sem.at[c])
        copy.start()
        copies.append(copy)
    for copy in copies:
        copy.wait()


def correlate(blocks, other):
    vmem = pl.BlockSpec(memory_space=pltpu.VMEM)
    return pl.pallas_call(
        correlate_kernel,
        out_shape=jax.ShapeDtypeStruct((CH_DEV, 2, 2 * LANES * Q_DEV, 8 * ROWS), jnp.bfloat16),
        in_specs=[vmem] * (ROWS + 1),
        out_specs=pl.BlockSpec(memory_space=pltpu.HBM),
        scratch_shapes=[
            pltpu.VMEM((2, Q_DEV, 8 * ROWS, 2 * SPECTRA), jnp.bfloat16),
            pltpu.VMEM((2, 2, P_DEV * PITCH, 8 * ROWS), jnp.float32),
            pltpu.VMEM((CH_DEV, 2, 2 * LANES * Q_DEV, 8 * ROWS), jnp.bfloat16),
            pltpu.SemaphoreType.DMA((CH_DEV,)),
        ],
        compiler_params=pltpu.CompilerParams(vmem_limit_bytes=32 << 20),
        name="correlate",
    )(*blocks, other)


def per_device(voltages, lane_map, input_flags):
    own = channelise(voltages, lane_map, input_flags)
    products = correlate(*gather(own))
    return products.reshape(CH_DEV, 2, P_DEV, 2 * Q_DEV, Q_DEV, P_DEV * ROWS)


def solution(mesh):
    fast = mesh.shape["row"] == ROWS and mesh.shape["col"] == 2 and mesh.shape["chan"] == 1
    return jax.shard_map(
        per_device if fast else per_device_general,
        mesh=mesh,
        in_specs=(P("row", ("col", "chan"), None), P("row", "col", None), P("row", "col")),
        out_specs=P("chan", None, "row", None, "col", None),
        check_vma=False,
    )
```

```python
import jax
import jax.experimental.pallas as pl
import jax.experimental.pallas.tpu as pltpu
import jax.numpy as jnp
import ml_dtypes
import numpy as np
from jax import lax
from jax.sharding import PartitionSpec as P

NFFT = 2048
TAPS = 4
P_DEV = 8
Q_DEV = 4
CH_DEV = 16
SPECTRA = 64
LANES = 32
FRAMES = 67
CHUNK = 128
CHUNKS = NFFT // CHUNK
ROWS = 16


def kernel_table(nfft, taps, chans):
    length = taps * nfft
    position = jnp.arange(length, dtype=jnp.float32)
    centre = (position - length / 2 + 0.5) / nfft
    window = jnp.sinc(centre) * (0.5 - 0.5 * jnp.cos(2.0 * jnp.pi * (position + 0.5) / length))
    norm_scale = jnp.sqrt(2.0 / jnp.sum(window * window))
    window = (window * norm_scale).reshape(taps, nfft)
    sample = jnp.arange(nfft, dtype=jnp.int32)
    bin_index = nfft // 4 + jnp.arange(chans, dtype=jnp.int32)
    phase_index = bin_index[:, None] * sample[None, :] % nfft
    phases = phase_index.astype(jnp.float32) * (2.0 * jnp.pi / nfft)
    both_parts = jnp.stack([jnp.cos(phases).T, -jnp.sin(phases).T], -1)
    built = window.T[:, :, None, None] * both_parts[:, None, :, :]
    return built.reshape(nfft, taps * chans * 2).astype(jnp.bfloat16)


def per_device_general(voltages, lane_map, input_flags):
    all_chans = CH_DEV * lax.axis_size("chan")
    half_q = voltages.shape[1]
    table_rows = kernel_table(NFFT, TAPS, all_chans)
    frames = voltages.reshape(P_DEV, half_q, FRAMES, NFFT)
    frame_sums = jnp.einsum("pqfn,nk->pqfk", frames, table_rows, preferred_element_type=jnp.float32)
    frame_sums = frame_sums.reshape(P_DEV, half_q, FRAMES, TAPS, all_chans, 2)
    tap_sum = frame_sums[:, :, 0:SPECTRA, 0]
    for tap_idx in range(1, TAPS):
        tap_sum = tap_sum + frame_sums[:, :, tap_idx : tap_idx + SPECTRA, tap_idx]
    filtered = tap_sum.astype(jnp.bfloat16)
    filtered = filtered.transpose(3, 0, 1, 4, 2).reshape(all_chans, P_DEV, half_q, 2 * SPECTRA)
    turned_over = lax.all_to_all(filtered, "chan", split_axis=0, concat_axis=2, tiled=True)
    lane_rows = turned_over.reshape(CH_DEV, LANES, 2 * SPECTRA)
    lane_index = lane_map.reshape(LANES)
    selector = (lane_index[:, None] == jnp.arange(LANES, dtype=jnp.int32)[None, :]).astype(
        jnp.bfloat16
    )
    reordered = jnp.einsum("kl,clz->ckz", selector, lane_rows, preferred_element_type=jnp.float32)
    weights = input_flags.reshape(LANES).astype(jnp.float32)[None, :, None]
    channelised = (
        (reordered * weights).astype(jnp.bfloat16).reshape(CH_DEV, P_DEV, Q_DEV, 2 * SPECTRA)
    )
    row_group = lax.all_gather(channelised, "col", axis=2, tiled=True)
    grid_cols = row_group.shape[2]
    row_block = row_group.reshape(CH_DEV, P_DEV * grid_cols, 2 * SPECTRA)
    col_set = lax.all_gather(channelised, "row", axis=1, tiled=True)
    real_part = col_set[..., :SPECTRA]
    imag_part = col_set[..., SPECTRA:]
    turned = jnp.concatenate([-imag_part, real_part], axis=-1)
    col_block = jnp.stack([col_set, turned], axis=1)
    products = jnp.einsum(
        "cik,crpqk->criqp", row_block, col_block, preferred_element_type=jnp.float32
    )
    products = (products * (1.0 / SPECTRA)).astype(jnp.bfloat16)
    return products.reshape(CH_DEV, 2, P_DEV, grid_cols, Q_DEV, col_set.shape[1])


PITCH = 36


def filter_table(chans):
    f32 = np.float32
    length = TAPS * NFFT
    position = np.arange(length, dtype=f32)
    centre = (position - f32(length / 2) + f32(0.5)) / f32(NFFT)
    window = np.sinc(centre.astype(np.float64)).astype(f32)
    window = window * (f32(0.5) - f32(0.5) * np.cos(f32(2.0 * np.pi) * (position + f32(0.5)) / f32(length)))
    window = (window * np.sqrt(f32(2.0) / np.sum(window * window))).reshape(TAPS, NFFT)
    bins = NFFT // 4 + np.arange(chans)
    phase_index = np.arange(NFFT)[:, None] * bins[None, :] % NFFT
    phases = phase_index.astype(f32) * f32(2.0 * np.pi / NFFT)
    parts = np.stack([np.cos(phases), -np.sin(phases)], 1)
    table = window.T[:, :, None, None] * parts[:, None]
    table = table.reshape(CHUNKS // 2, 2, CHUNK, TAPS * 2 * chans)
    return table.transpose(0, 2, 1, 3).reshape(NFFT // 2, -1).astype(ml_dtypes.bfloat16)


def filter_kernel(
    volts, table, lane_map, flags, out, held, table_v, map_s, flags_s, frames, sums, lanes, rows, in_sem, const_sem
):
    spans = ((0, 2), (2, 5), (5, 8))
    arrivals = [
        [
            pltpu.make_async_copy(
                volts.at[pl.ds(low, high - low), :, j],
                held.at[pl.ds(low, high - low), j, pl.ds(0, FRAMES)],
                in_sem.at[k],
            )
            for j in range(CHUNKS // 2)
        ]
        for k, (low, high) in enumerate(spans)
    ]
    get_table = pltpu.make_async_copy(table, table_v, const_sem.at[0])
    get_map = pltpu.make_async_copy(lane_map, map_s, const_sem.at[1])
    get_flags = pltpu.make_async_copy(flags, flags_s, const_sem.at[2])

    def begin(k):
        for copy in arrivals[k]:
            copy.start()
        if k == 0:
            get_table.start()
        if k == 1:
            get_map.start()
            get_flags.start()

    first_half = lax.broadcasted_iota(jnp.int32, (16, 8, CHUNK), 1) < Q_DEV
    real_lanes = lax.broadcasted_iota(jnp.int32, (CH_DEV, 2 * SPECTRA), 1) < SPECTRA
    lane_group = lax.broadcasted_iota(jnp.int32, (128, CHUNK), 1) // 32

    def pair(low, high):
        upper = first_half[: low.shape[0]]
        straight = jnp.where(upper, low[:, :, :CHUNK], high[:, :, CHUNK:])
        crossed = jnp.where(upper, high[:, :, :CHUNK], low[:, :, CHUNK:])
        return straight + pltpu.roll(crossed, 4, 1)

    def frames_of(p, i, kept):
        spans = [(128 * i, 128), (256 + 128 * i, 128 if i < 1 else 160)]
        block = jnp.concatenate(
            [
                jnp.concatenate([held.at[p, j].reshape(68 * 8, CHUNK)[at : at + size] for at, size in spans], axis=0)
                for j in range(CHUNKS // 2)
            ],
            axis=1,
        )
        both = jnp.dot(block, table_v[...], preferred_element_type=jnp.float32)
        both = both.reshape(-1, 8, 2 * CHUNK)
        frames[p % 2, 16 * i : 16 * i + 16] = pair(both[:16], both[16:32])
        if i == 0:
            kept = both[16:19]
        if i == 1:
            frames[p % 2, 32:35] = pair(kept, both[32:35])
        return kept

    def taps_of(p, i):
        total = None
        for tap in range(TAPS):
            term = frames[p % 2, 16 * i + tap : 16 * i + tap + 16]
            turn = 32 * (p % 4 - tap) % CHUNK
            if turn:
                term = pltpu.roll(term, turn, 2)
            total = term if total is None else total + term
        total = total.reshape(128, CHUNK)
        at = slice(128 * i, 128 * i + 128)
        sums[p // 4, at] = total if p % 4 == 0 else jnp.where(lane_group == p % 4, total, sums[p // 4, at])

    def finish(first):
        by_q = [
            sums[first // 4, pl.ds(half * Q_DEV + q, SPECTRA // 2, stride=8), :]
            for q in range(Q_DEV)
            for half in range(2)
        ]
        turned = jnp.concatenate(by_q, axis=0).T.reshape(4, 2, CH_DEV, Q_DEV * SPECTRA)
        for i in range(4):
            for q in range(Q_DEV):
                real, imag = (turned[i, part, :, q // 2 * CHUNK : q // 2 * CHUNK + CHUNK] for part in range(2))
                if q % 2:
                    real = pltpu.roll(real, SPECTRA, 1)
                else:
                    imag = pltpu.roll(imag, SPECTRA, 1)
                lanes[(first + i) * Q_DEV + q] = jnp.where(real_lanes, real, imag)

    for k in range(len(spans)):
        begin(k)
    for p in range(P_DEV):
        for k, (low, _) in enumerate(spans):
            if p == low:
                for copy in arrivals[k]:
                    copy.wait()
        if p == 0:
            get_table.wait()
        if p == 5:
            get_map.wait()
            get_flags.wait()
        kept = None
        for i in range(2):
            kept = frames_of(p, i, kept)
            if p > 0:
                taps_of(p - 1, i)
        if p == 5:
            finish(0)
    for i in range(2):
        taps_of(P_DEV - 1, i)
    finish(4)
    for p in range(P_DEV):
        for q in range(Q_DEV):
            weight = flags_s[q, p].astype(jnp.float32)
            rows[pl.ds(q * P_DEV + p, CH_DEV, stride=PITCH), :] = lanes[map_s[0, p * Q_DEV + q]] * weight
    for c in range(CH_DEV):
        out[c] = rows[PITCH * c : PITCH * c + LANES].astype(jnp.bfloat16)


def channelise(voltages, lane_map, input_flags):
    volts = voltages.reshape(P_DEV, Q_DEV, FRAMES, CHUNKS // 2, 2, CHUNK).transpose(0, 2, 3, 4, 1, 5)
    volts = volts.reshape(P_DEV, FRAMES, CHUNKS // 2, 2 * Q_DEV, CHUNK)
    vmem = pl.BlockSpec(memory_space=pltpu.VMEM)
    hbm = pl.BlockSpec(memory_space=pltpu.HBM)
    return pl.pallas_call(
        filter_kernel,
        out_shape=jax.ShapeDtypeStruct((CH_DEV, LANES, 2 * SPECTRA), jnp.bfloat16),
        in_specs=[hbm] * 4,
        out_specs=vmem,
        scratch_shapes=[
            pltpu.VMEM((P_DEV, CHUNKS // 2, 68, 2 * Q_DEV, CHUNK), jnp.bfloat16),
            pltpu.VMEM((NFFT // 2, 2 * CHUNK), jnp.bfloat16),
            pltpu.SMEM((1, LANES), jnp.int32),
            pltpu.SMEM((Q_DEV, P_DEV), jnp.int32),
            pltpu.VMEM((2, 35, 8, CHUNK), jnp.float32),
            pltpu.VMEM((2, 4 * SPECTRA, CHUNK), jnp.float32),
            pltpu.VMEM((LANES, CH_DEV, 2 * SPECTRA), jnp.float32),
            pltpu.VMEM((CH_DEV * PITCH, 2 * SPECTRA), jnp.float32),
            pltpu.SemaphoreType.DMA((3,)),
            pltpu.SemaphoreType.DMA((3,)),
        ],
        compiler_params=pltpu.CompilerParams(vmem_limit_bytes=56 << 20),
        name="channelise",
    )(
        volts,
        jnp.asarray(filter_table(CH_DEV)),
        lane_map.reshape(1, LANES),
        input_flags.T,
    )


def gather(own):
    def swap(block, d):
        return lax.ppermute(block, "row", [(i, i ^ d) for i in range(ROWS)])

    blocks = {0: own}
    for d in (8, 4, 2, 6):
        blocks[d] = swap(own, d)
    for d in (14, 12, 10):
        blocks[d] = swap(blocks[8], d ^ 8)
    for d in range(0, ROWS, 2):
        blocks[d + 1] = swap(blocks[d], 1)
    late, _ = lax.optimization_barrier((own, blocks[8]))
    other = lax.ppermute(late, "col", [(0, 1), (1, 0)])
    back, _ = lax.optimization_barrier((blocks[1], blocks[6]))
    blocks[0] = swap(back, 1)
    return [blocks[d] for d in range(ROWS)], other


def correlate_kernel(*refs):
    blocks, other = refs[:ROWS], refs[ROWS]
    out, columns, spread, packed, sem = refs[ROWS + 1 :]
    row = lax.axis_index("row")
    first_col = lax.axis_index("col") == 0
    odd = lax.rem(row, 2) == 1
    pair = lax.div(row, 2)
    sign = jnp.where(lax.broadcasted_iota(jnp.int32, (64, 128), 1) < SPECTRA, 1.0, -1.0)
    sign = sign.astype(jnp.bfloat16)
    copies = []
    for c in range(CH_DEV):
        slot = c % 2
        for e in range(ROWS // 2):
            near, far = blocks[2 * e][c], blocks[2 * e + 1][c]
            low, high = jnp.where(odd, far, near), jnp.where(odd, near, far)
            at = pl.multiple_of(lax.bitwise_xor(pair, e) * 16, 16)
            for q in range(Q_DEV):
                both = jnp.concatenate([low[q * 8 : q * 8 + 8], high[q * 8 : q * 8 + 8]], axis=0)
                columns[slot, q, pl.ds(at, 16), :] = both
        mine, theirs = blocks[0][c], other[c]
        left = jnp.concatenate(
            [jnp.where(first_col, mine, theirs), jnp.where(first_col, theirs, mine)], axis=0
        )
        left = jnp.concatenate([left, pltpu.roll(left, SPECTRA, 1) * sign], axis=0)
        for h in range(2):
            right = columns[slot, 2 * h : 2 * h + 2].reshape(256, 2 * SPECTRA)
            products = lax.dot_general(
                left, right, (((1,), (1,)), ((), ())), preferred_element_type=jnp.float32
            ) * (1.0 / SPECTRA)
            for k in range(2):
                for part in range(2):
                    for q in range(2 * Q_DEV):
                        start = (part * 8 + q) * 8
                        spread[slot, part, pl.ds(q * Q_DEV + 2 * h + k, 8, stride=PITCH), :] = products[
                            start : start + 8, k * 128 : k * 128 + 128
                        ]
        for p in range(P_DEV):
            packed[c, :, 32 * p : 32 * p + 32] = spread[slot, :, PITCH * p : PITCH * p + 32].astype(jnp.bfloat16)
        copy = pltpu.make_async_copy(packed.at[c], out.at[c], sem.at[c])
        copy.start()
        copies.append(copy)
    for copy in copies:
        copy.wait()


def correlate(blocks, other):
    vmem = pl.BlockSpec(memory_space=pltpu.VMEM)
    return pl.pallas_call(
        correlate_kernel,
        out_shape=jax.ShapeDtypeStruct((CH_DEV, 2, 2 * LANES * Q_DEV, 8 * ROWS), jnp.bfloat16),
        in_specs=[vmem] * (ROWS + 1),
        out_specs=pl.BlockSpec(memory_space=pltpu.HBM),
        scratch_shapes=[
            pltpu.VMEM((2, Q_DEV, 8 * ROWS, 2 * SPECTRA), jnp.bfloat16),
            pltpu.VMEM((2, 2, P_DEV * PITCH, 8 * ROWS), jnp.float32),
            pltpu.VMEM((CH_DEV, 2, 2 * LANES * Q_DEV, 8 * ROWS), jnp.bfloat16),
            pltpu.SemaphoreType.DMA((CH_DEV,)),
        ],
        compiler_params=pltpu.CompilerParams(vmem_limit_bytes=32 << 20),
        name="correlate",
    )(*blocks, other)


def per_device(voltages, lane_map, input_flags):
    own = channelise(voltages, lane_map, input_flags)
    products = correlate(*gather(own))
    return products.reshape(CH_DEV, 2, P_DEV, 2 * Q_DEV, Q_DEV, P_DEV * ROWS)


def solution(mesh):
    fast = mesh.shape["row"] == ROWS and mesh.shape["col"] == 2 and mesh.shape["chan"] == 1
    return jax.shard_map(
        per_device if fast else per_device_general,
        mesh=mesh,
        in_specs=(P("row", ("col", "chan"), None), P("row", "col", None), P("row", "col")),
        out_specs=P("chan", None, "row", None, "col", None),
        check_vma=False,
    )
```
